256 devices in a mesh: scen: 16 (over x, z_lo, core), path: 16 (over z_hi, y).
Axes of the slice: x: 4, y: 4, z: 8 (z_hi: 4, z_lo: 2; z = z_hi * 2 + z_lo), core: 2. Of those that a mesh axis runs over, the one named last changes fastest.
Arguments:
- increments: bfloat16 [16, 32, 1024, 2048], P(None, None, 'path', 'scen'), may hold values from -12 to 12
- outer_shock: float32 [32, 2048], P(None, ('scen', 'path')), may hold values from -5 to 5
- outer_vol: float32 [32], replicated, may hold values from 0.1 to 0.4
- factor_vol: float32 [32], replicated, may hold values from 0.1 to 0.5
- factor_mix: float32 [32, 32], replicated, may hold values from -1 to 1
- leg_factor: int32 [64, 4], replicated, may hold values from 0 to 31
- leg_weight: float32 [64, 4], replicated, may hold values from 0.2 to 0.8
- strike: float32 [64], replicated, may hold values from 1.2 to 2.4
- reserve: float32 [2048, 64], P(('scen', 'path')), may hold values from 0 to 0.6
Outputs:
- fine_excess: float32 [2048, 64], P(('scen', 'path'))
- correction: float32 [2048, 64], P(('scen', 'path'))
The draws below stay inside these ranges and needn't reach their ends.
All inputs are finite; a program needn't handle non-finite values.
Results may differ from the reference program's by a relative error of at most 0.0003.
Values sent between devices are 32-bit elements; how exact they have to be, the bound alone decides.
No kernel may reach another device: no remote copies, remote signals or barrier semaphores. Data moves between devices by JAX's collectives and lax.ppermute only.
A program may use at most 64 MiB of HBM per device.

```python
import math
import jax
import jax.numpy as jnp
from jax import lax

FACTORS = 32
PRODUCTS = 64
LEGS = 4
STEPS = 16
PATHS = 1024
SC_DEV = 128
SCEN = 2048
N_SCEN = 16


def draw_increments(key, part):
    key = jax.random.fold_in(key, 11)
    base_key, half_key, step_key = jax.random.split(key, 3)
    half_scale = jnp.exp(jax.random.uniform(half_key, (2, SCEN), jnp.float32, -1.0, 0.7))
    step_scale = jnp.exp(jax.random.uniform(step_key, (STEPS, SCEN), jnp.float32, -0.4, 0.4))
    path_half = (jnp.arange(PATHS, dtype=jnp.int32) >= PATHS // 2).astype(jnp.int32)
    path_scale = jnp.where(path_half[:, None] == 0, half_scale[0][None, :], half_scale[1][None, :])

    def one_step(step_index):
        step_key_now = jax.random.fold_in(base_key, step_index)
        base = jax.random.truncated_normal(step_key_now, -4.0, 4.0, (FACTORS, PATHS, SCEN), jnp.float32)
        scale_now = lax.dynamic_index_in_dim(step_scale, step_index, 0, keepdims=False)
        return (base * path_scale[None, :, :] * scale_now[None, None, :]).astype(jnp.bfloat16)
    return lax.map(one_step, jnp.arange(STEPS, dtype=jnp.int32))


def touch_ends(drawn, own_key, low, top_value):
    longest = drawn.shape.index(max(drawn.shape))
    spots = []
    for shift in (0, 1):
        where = [jax.random.randint(jax.random.fold_in(own_key, axis), (), 0, length) for axis, length in enumerate(drawn.shape)]
        where[longest] = (where[longest] + shift) % drawn.shape[longest]
        spots.append(tuple(where))
    return drawn.at[spots[0]].set(low).at[spots[1]].set(top_value)


def block_levels(own_key, extent, shards, low, high):
    factor_of, own = 1.0, jax.random.fold_in(own_key, 6)
    for position, parts in shards:
        draws = jnp.exp(jax.random.uniform(jax.random.fold_in(own, position), (parts,), jnp.float32, low / len(shards), high / len(shards)))
        factor_of = factor_of * jnp.repeat(draws, extent[position] // parts).reshape([-1 if axis == position else 1 for axis in range(len(extent))])
    return factor_of


def noise(key, shape, width, most, cuts=(), kind=jnp.bfloat16):
    loudness = block_levels(key, shape, cuts, -0.22, 0.18) if cuts else 1.0
    drawn = jax.random.normal(key, shape, jnp.float32) * width * loudness
    return jnp.minimum(jnp.maximum(drawn, -most), most).astype(kind)


def setup_inputs(seed: int = 0) -> dict:
    streams_of = jax.random.split(jax.random.key(seed), 10)
    increments = draw_increments(jax.random.fold_in(streams_of[9], 71), 0)
    outer_shock = noise(streams_of[1], (FACTORS, SCEN), 1.0, 5.0, ((1, 256),), jnp.float32)
    outer_vol = jnp.clip(jnp.exp(jax.random.uniform(streams_of[2], (FACTORS,), jnp.float32, math.log(0.1), math.log(0.4))), 0.1, 0.4)
    factor_vol = jnp.clip(jnp.exp(jax.random.uniform(streams_of[3], (FACTORS,), jnp.float32, math.log(0.1), math.log(0.5))), 0.1, 0.5)
    factor_mix = noise(streams_of[4], (FACTORS, FACTORS), FACTORS ** -0.5, 1.0, (), jnp.float32)
    leg_factor = touch_ends(jax.random.randint(streams_of[5], (PRODUCTS, LEGS), 0, FACTORS), jax.random.fold_in(streams_of[5], 1), 0, FACTORS - 1).astype(jnp.int32)
    leg_weight = jnp.clip(jax.random.uniform(streams_of[6], (PRODUCTS, LEGS), jnp.float32, 0.2, 0.8), 0.2, 0.8)
    strike = jnp.clip(jax.random.uniform(streams_of[7], (PRODUCTS,), jnp.float32, 1.2, 2.4), 1.2, 2.4)
    reserve = jnp.clip(0.6 * jax.random.uniform(streams_of[8], (SCEN, PRODUCTS), jnp.float32) ** block_levels(streams_of[8], (SCEN, PRODUCTS), ((0, 256),), -0.2, 0.2), 0.0, 0.6)
    return dict(increments=increments, outer_shock=outer_shock, outer_vol=outer_vol, factor_vol=factor_vol, factor_mix=factor_mix, leg_factor=leg_factor, leg_weight=leg_weight, strike=strike, reserve=reserve)


def build_exposure(leg_factor, leg_weight):
    factor_ids = jnp.arange(FACTORS, dtype=jnp.int32)
    matches = (leg_factor[None, :, :] == factor_ids[:, None, None]).astype(jnp.float32)
    return jnp.sum(leg_weight[None, :, :] * matches, axis=2)


def reference(increments, outer_shock, outer_vol, factor_vol, factor_mix, leg_factor, leg_weight, strike, reserve):
    exposure = build_exposure(leg_factor, leg_weight)
    start = outer_vol[:, None] * outer_shock
    time_step = 1.0 / STEPS
    root_step = time_step ** 0.5

    def one_block(block_index):
        offset = (block_index * SC_DEV).astype(jnp.int32)
        normals_all = lax.dynamic_slice_in_dim(increments, offset, SC_DEV, 3)
        begin = lax.dynamic_slice_in_dim(start, offset, SC_DEV, 1)
        level_init = jnp.broadcast_to(begin[:, None, :], (FACTORS, PATHS, SC_DEV)).astype(jnp.float32)

        def advance(log_level, normals):
            shock = jnp.einsum("kl,lps->kps", factor_mix, normals.astype(jnp.float32), precision=lax.Precision.HIGHEST)
            local_vol = factor_vol[:, None, None] * (1.0 + 0.5 * jnp.tanh(log_level))
            log_level = log_level - 0.5 * local_vol * local_vol * time_step + local_vol * root_step * shock
            values = jnp.einsum("kj,kps->jps", exposure, jnp.exp(log_level), precision=lax.Precision.HIGHEST)
            payoff = jnp.maximum(values - strike[:, None, None], 0.0)
            halves = jnp.sum(payoff.reshape(PRODUCTS, 2, PATHS // 2, SC_DEV), axis=2)
            return log_level, halves

        unused, halves = lax.scan(advance, level_init, normals_all)
        first_half = halves[:, :, 0, :] / (PATHS // 2)
        second_half = halves[:, :, 1, :] / (PATHS // 2)
        fine = (halves[:, :, 0, :] + halves[:, :, 1, :]) / PATHS
        limit = lax.dynamic_slice_in_dim(reserve, offset, SC_DEV, 0).T[None]
        fine_hinge = jnp.maximum(fine - limit, 0.0)
        coarse = 0.5 * (jnp.maximum(first_half - limit, 0.0) + jnp.maximum(second_half - limit, 0.0))
        return jnp.mean(fine_hinge, axis=0).T, jnp.mean(fine_hinge - coarse, axis=0).T

    fine_blocks, corr_blocks = lax.map(one_block, jnp.arange(N_SCEN, dtype=jnp.int32))
    return fine_blocks.reshape(SCEN, PRODUCTS), corr_blocks.reshape(SCEN, PRODUCTS)
```

```python
import functools
import jax
import jax.numpy as jnp
from jax import lax
from jax.experimental import pallas as pl
from jax.experimental.pallas import tpu as pltpu
from jax.sharding import PartitionSpec as P

SUB = 8


def build_exposure(leg_factor, leg_weight, factor_count):
    factor_ids = jnp.arange(factor_count, dtype=jnp.int32)
    matches = (leg_factor[None, :, :] == factor_ids[:, None, None]).astype(jnp.float32)
    return jnp.sum(leg_weight[None, :, :] * matches, axis=2)


def split_two(full):
    high = full.astype(jnp.bfloat16)
    low = (full - high.astype(jnp.float32)).astype(jnp.bfloat16)
    return high, low


def split_weights(full):
    high = lax.reduce_precision(full, 8, 7)
    low = lax.reduce_precision(full - high, 8, 7)
    return high.astype(jnp.bfloat16), low.astype(jnp.bfloat16)


def block_diag(block, copies):
    eye = jnp.eye(copies, dtype=block.dtype)
    rows, cols = block.shape
    return (eye[:, None, :, None] * block[None, :, None, :]).reshape(copies * rows, copies * cols)


def simulate_kernel(
    step_total, inc_ref, begin_ref, mix_ref, val_ref, drift_ref, strike_ref, out_ref, level, buf, sums
):
    step = pl.program_id(0)
    factors, paths, scen = inc_ref.shape[1:]
    products = strike_ref.shape[0]
    groups = paths // SUB

    @pl.when(step == 0)
    def _():
        begin = begin_ref[...]
        for path in range(paths):
            level[path] = begin

    drift = drift_ref[...]
    strike = strike_ref[...]
    acc = strike * (-1.0 * paths)
    for group in range(groups):
        chunk = inc_ref[0, :, pl.ds((group // 2) * 2 * SUB, 2 * SUB), :].astype(jnp.float32)
        buf[group] = chunk[:, (group % 2) * SUB : (group % 2 + 1) * SUB, :].reshape(
            factors * SUB, scen
        )
        cols = []
        for path in range(SUB):
            rows = buf[group, pl.ds(path, factors, stride=SUB), :].astype(jnp.bfloat16)
            cols.append(rows)
        half = SUB // 2
        left = jnp.concatenate([c for c in cols[:half] for _ in range(2)], axis=0)
        right = jnp.concatenate([c for c in cols[half:] for _ in range(2)], axis=0)
        normals = jnp.concatenate([left, right], axis=1)
        shock = jnp.dot(mix_ref[...], normals, preferred_element_type=jnp.float32)
        pieces = []
        for path in range(SUB):
            row = (path % half) * factors
            col = (path // half) * scen
            part = shock[row : row + factors, col : col + scen]
            old = level[group * SUB + path]
            wide = jnp.tanh(old) + 2.0
            new = old + wide * (part - drift * wide)
            level[group * SUB + path] = new
            grown = jnp.exp(new)
            high, low = split_two(grown)
            pieces.append(jnp.concatenate([high, low, high], axis=0))
        for quad in range(SUB // 4):
            four = pieces[quad * 4 : quad * 4 + 4]
            operand = jnp.concatenate(
                [jnp.concatenate(four[:2], axis=0), jnp.concatenate(four[2:], axis=0)], axis=1
            )
            values = jnp.dot(val_ref[...], operand, preferred_element_type=jnp.float32)
            for path in range(4):
                row = (path % 2) * products
                col = (path // 2) * scen
                acc = acc + jnp.maximum(values[row : row + products, col : col + scen], strike)
    sums[pl.ds(pl.multiple_of(step * products, products), products), :] = acc

    @pl.when(step == step_total - 1)
    def _():
        out_ref[...] = jnp.transpose(sums[...])


def simulate(increments, begin, mix_w, val_w, drift, strike):
    steps, factors, paths, scen = increments.shape
    products = strike.shape[0]
    whole = lambda a: pl.BlockSpec(a.shape, lambda t: (0,) * a.ndim)
    return pl.pallas_call(
        functools.partial(simulate_kernel, steps),
        grid=(steps,),
        out_shape=jax.ShapeDtypeStruct((scen, steps * products), jnp.float32),
        in_specs=[
            pl.BlockSpec((1, factors, paths, scen), lambda t: (t, 0, 0, 0)),
            whole(begin),
            whole(mix_w),
            whole(val_w),
            whole(drift),
            whole(strike),
        ],
        out_specs=pl.BlockSpec((scen, steps * products), lambda t: (0, 0)),
        scratch_shapes=[
            pltpu.VMEM((paths, factors, scen), jnp.float32),
            pltpu.VMEM((paths // SUB, factors * SUB, scen), jnp.float32),
            pltpu.VMEM((steps * products, scen), jnp.float32),
        ],
        compiler_params=pltpu.CompilerParams(vmem_limit_bytes=32 * 1024 * 1024),
        name="simulate",
    )(increments, begin, mix_w, val_w, drift, strike)


def finish_kernel(paths_total, parts_ref, reserve_ref, fine_ref, corr_ref):
    count = parts_ref.shape[0]
    rows, products = reserve_ref.shape
    width = parts_ref.shape[2]
    first = parts_ref[0]
    second = parts_ref[count // 2]
    for src in range(1, count // 2):
        first = first + parts_ref[src]
        second = second + parts_ref[count // 2 + src]
    reserve = reserve_ref[...]
    limit = jnp.concatenate([reserve] * (width // products), axis=1)
    scale = 1.0 / paths_total
    fine = jnp.maximum((first + second) * scale - limit, 0.0)
    coarse = 0.5 * (
        jnp.maximum(first * (2.0 * scale) - limit, 0.0)
        + jnp.maximum(second * (2.0 * scale) - limit, 0.0)
    )
    gap = fine - coarse

    def over_steps(term):
        lanes = 2 * products
        total = term[:, :lanes]
        for start in range(lanes, width, lanes):
            total = total + term[:, start : start + lanes]
        return (total[:, :products] + total[:, products:]) * (products / width)

    fine_ref[...] = over_steps(fine)
    corr_ref[...] = over_steps(gap)


def per_device(
    increments,
    outer_shock,
    outer_vol,
    factor_vol,
    factor_mix,
    leg_factor,
    leg_weight,
    strike,
    reserve,
):
    factor_count = factor_mix.shape[0]
    product_count = strike.shape[0]
    step_count, _, paths_here, scen_rows = increments.shape
    path_count = lax.axis_size("path")
    paths_total = paths_here * path_count
    row_count = scen_rows // path_count

    own = (outer_vol[:, None] * outer_shock).T
    spread = jnp.broadcast_to(own[None], (path_count, row_count, factor_count))
    begin_rows = lax.all_to_all(spread, "path", 0, 0, tiled=True)
    begin = begin_rows.reshape(scen_rows, factor_count).T

    root_step = (1.0 / step_count) ** 0.5
    half_vol = 0.5 * root_step * factor_vol
    drift = jnp.broadcast_to((0.5 * half_vol * half_vol)[:, None], (factor_count, scen_rows))
    mix_high, mix_low = split_weights(half_vol[:, None] * factor_mix)
    mix_w = block_diag(jnp.concatenate([mix_high, mix_low], axis=1), SUB // 2)
    exposure = build_exposure(leg_factor, leg_weight, factor_count).T
    val_high, val_low = split_weights(exposure)
    val_w = block_diag(jnp.concatenate([val_high, val_high, val_low], axis=1), 2)
    strike_wide = jnp.broadcast_to(strike[:, None], (product_count, scen_rows))

    local = simulate(increments, begin, mix_w, val_w, drift, strike_wide)
    parts = lax.all_to_all(
        local.reshape(path_count, row_count, step_count * product_count), "path", 0, 0, tiled=True
    )
    out = jax.ShapeDtypeStruct((row_count, product_count), jnp.float32)
    return pl.pallas_call(
        functools.partial(finish_kernel, paths_total), out_shape=(out, out), name="finish"
    )(parts, reserve)


def solution(mesh):
    in_specs = (
        P(None, None, "path", "scen"),
        P(None, ("scen", "path")),
        P(),
        P(),
        P(),
        P(),
        P(),
        P(),
        P(("scen", "path"), None),
    )
    out_specs = (P(("scen", "path"), None), P(("scen", "path"), None))
    return jax.shard_map(
        per_device, mesh=mesh, in_specs=in_specs, out_specs=out_specs, check_vma=False
    )
```

```python
import functools
import jax
import jax.numpy as jnp
from jax import lax
from jax.experimental import pallas as pl
from jax.experimental.pallas import tpu as pltpu
from jax.sharding import PartitionSpec as P

SUB = 8
NEAR = 4
CHUNKS = (10, 6)
STEPS_PER_BLOCK = 2
VMEM_BYTES = 50 * 1024 * 1024


def split_two(full):
    high = full.astype(jnp.bfloat16)
    low = (full - high.astype(jnp.float32)).astype(jnp.bfloat16)
    return high, low


def iota(shape, dim):
    return lax.broadcasted_iota(jnp.int32, shape, dim)


def prepare_kernel(
    root_step,
    scen,
    vol_ref,
    base_ref,
    mix_ref,
    leg_ref,
    weight_ref,
    strike_ref,
    mix_out,
    val_out,
    drift_out,
    strike_out,
    scale_out,
):
    factors = mix_ref.shape[0]
    products, legs = leg_ref.shape
    same = iota((factors, factors), 0) == iota((factors, factors), 1)
    column = lambda row, pick: jnp.sum(jnp.where(pick, row, 0.0), axis=1, keepdims=True)
    half_vol = column(base_ref[...], same) * (0.5 * root_step)
    drift_out[...] = jnp.broadcast_to(0.5 * half_vol * half_vol, (factors, scen))
    scale_out[...] = jnp.broadcast_to(column(vol_ref[...], same), (factors, scen))
    square = iota((products, products), 0) == iota((products, products), 1)
    strike_out[...] = jnp.broadcast_to(column(strike_ref[...], square), (products, scen))

    high, low = split_two(half_vol * mix_ref[...])
    wide = factors * SUB
    spread = (iota((factors, wide), 0) == iota((factors, wide), 1) // SUB).astype(jnp.bfloat16)
    rows = jnp.concatenate(
        [
            jnp.dot(high, spread, preferred_element_type=jnp.float32),
            jnp.dot(low, spread, preferred_element_type=jnp.float32),
        ],
        axis=0,
    )
    for path in range(SUB):
        keep = iota((2 * factors, wide), 1) % SUB == path
        mix_out[path * 2 * factors : (path + 1) * 2 * factors, :] = jnp.where(
            keep, rows, 0.0
        ).astype(jnp.bfloat16)

    ids = iota((products, factors), 1)
    exposure = jnp.zeros((products, factors), jnp.float32)
    for leg in range(legs):
        hit = leg_ref[:, leg : leg + 1] == ids
        exposure = exposure + jnp.where(hit, weight_ref[:, leg : leg + 1], 0.0)
    high, low = split_two(exposure)
    span = 2 * 3 * factors
    lane = iota((factors, span), 1)
    match = iota((factors, span), 0) == lane % factors
    third = (lane // factors) % 3
    put_high = jnp.logical_and(match, third != 2).astype(jnp.bfloat16)
    put_low = jnp.logical_and(match, third == 2).astype(jnp.bfloat16)
    weights = jnp.dot(high, put_high, preferred_element_type=jnp.float32) + jnp.dot(
        low, put_low, preferred_element_type=jnp.float32
    )
    block = iota((products, span), 1) // (3 * factors)
    for path in range(2):
        val_out[path * products : (path + 1) * products, :] = jnp.where(
            block == path, weights, 0.0
        ).astype(jnp.bfloat16)


def prepare(root_step, scen, outer_vol, factor_vol, factor_mix, leg_factor, leg_weight, strike):
    factors = factor_mix.shape[0]
    products = strike.shape[0]
    shapes = (
        ((2 * SUB * factors, SUB * factors), jnp.bfloat16),
        ((2 * products, 6 * factors), jnp.bfloat16),
        ((factors, scen), jnp.float32),
        ((products, scen), jnp.float32),
        ((factors, scen), jnp.float32),
    )
    return pl.pallas_call(
        functools.partial(prepare_kernel, root_step, scen),
        out_shape=tuple(jax.ShapeDtypeStruct(s, d) for s, d in shapes),
        cost_estimate=pl.CostEstimate(flops=20_000_000, bytes_accessed=1_000_000, transcendentals=0),
        name="prepare",
    )(
        outer_vol.reshape(1, factors),
        factor_vol.reshape(1, factors),
        factor_mix,
        leg_factor,
        leg_weight,
        strike.reshape(1, products),
    )


def run_steps(inc_ref, mix_ref, val_ref, drift, strike, level, sums, first_row):
    block_steps, factors, paths, scen = inc_ref.shape
    products = strike.shape[0]
    unit = 2 * SUB
    units = [(step, start) for step in range(block_steps) for start in range(0, paths, unit)]

    def shock_of(step, start):
        chunk = inc_ref[step, :, start : start + unit, :].astype(jnp.float32)
        halves = [
            chunk[:, side * SUB : (side + 1) * SUB, :].reshape(factors * SUB, scen)
            for side in range(2)
        ]
        normals = jnp.concatenate([h.astype(jnp.bfloat16) for h in halves], axis=1)
        return jnp.dot(mix_ref[...], normals, preferred_element_type=jnp.float32)

    def grow(shock, start, path, side):
        row = path * 2 * factors
        cols = slice(side * scen, (side + 1) * scen)
        part = shock[row : row + factors, cols] + shock[row + factors : row + 2 * factors, cols]
        place = start + side * SUB + path
        old = level[place]
        wide = jnp.tanh(old) + 2.0
        new = old + wide * (part - drift * wide)
        level[place] = new
        high, low = split_two(jnp.exp(new))
        return jnp.concatenate([high, low, high], axis=0)

    def fold(acc, values):
        for path in range(2):
            for side in range(2):
                piece = values[
                    path * products : (path + 1) * products, side * scen : (side + 1) * scen
                ]
                acc = acc + jnp.maximum(piece, strike)
        return acc

    waiting = None
    acc = None
    shock = shock_of(*units[0])
    for index, (step, start) in enumerate(units):
        ahead = shock_of(*units[index + 1]) if index + 1 < len(units) else None
        for pair in range(SUB // 2):
            sides = []
            for side in range(2):
                sides.append(
                    jnp.concatenate(
                        [grow(shock, start, 2 * pair + path, side) for path in range(2)], axis=0
                    )
                )
            operand = jnp.concatenate(sides, axis=1)
            values = jnp.dot(val_ref[...], operand, preferred_element_type=jnp.float32)
            if waiting is not None:
                acc = fold(acc, waiting)
            if start == 0 and pair == 0:
                if acc is not None:
                    sums[pl.ds(first_row + (step - 1) * products, products), :] = acc
                acc = strike * (-1.0 * paths)
            waiting = values
        shock = ahead
    acc = fold(acc, waiting)
    sums[pl.ds(first_row + (block_steps - 1) * products, products), :] = acc


def send_blocks(spot, result, out_refs):
    near = lax.rem(spot, NEAR)
    rows = result.shape[0] // out_refs[0].shape[0]
    far = out_refs[0].shape[0] // SUB
    for turn, out_ref in enumerate(out_refs):
        other = jnp.bitwise_xor(near, turn)
        for place in range(far):
            begin = pl.multiple_of((place * rows + other) * SUB, SUB)
            out_ref[place * SUB : (place + 1) * SUB, :] = result[pl.ds(begin, SUB), :]


def simulate_kernel(first, last, blocks, spot_ref, inc_ref, *refs):
    if first:
        stacks, refs = refs[:NEAR], refs[NEAR:]
        scale_ref, refs = refs[0], refs[1:]
    else:
        level_in, refs = refs[0], refs[1:]
    mix_ref, val_ref, drift_ref, strike_ref = refs[:4]
    out_refs, refs = refs[4 : 4 + NEAR], refs[4 + NEAR :]
    level, sums, result = refs
    block = pl.program_id(0)
    block_steps, factors, paths, scen = inc_ref.shape
    products = strike_ref.shape[0]
    spot = spot_ref[0]

    @pl.when(block == 0)
    def _():
        if first:
            near = lax.rem(spot, NEAR)
            far = lax.div(spot, NEAR)
            for across, stack in enumerate(stacks):
                for turn in range(NEAR):
                    source = jnp.bitwise_xor(far, across) * NEAR + jnp.bitwise_xor(near, turn)
                    begin = pl.multiple_of(source * SUB, SUB)
                    result[pl.ds(begin, SUB), 0:factors] = stack[turn]
            start = jnp.transpose(result[:, 0:scen])[0:factors, :] * scale_ref[...]
            for path in range(paths):
                level[path] = start
        else:
            for path in range(paths):
                level[path] = level_in[path]

    run_steps(
        inc_ref,
        mix_ref,
        val_ref,
        drift_ref[...],
        strike_ref[...],
        level,
        sums,
        pl.multiple_of(block * block_steps * products, products),
    )

    @pl.when(block == blocks - 1)
    def _():
        result[...] = jnp.transpose(sums[...])
        send_blocks(spot, result, out_refs)


def simulate(begin_step, steps, last, spot, increments, state, weights):
    _, factors, paths, scen = increments.shape
    products = weights[3].shape[0]
    first = begin_step == 0
    blocks = steps // STEPS_PER_BLOCK
    offset = begin_step // STEPS_PER_BLOCK
    whole = lambda a: pl.BlockSpec(a.shape, lambda t: (0,) * a.ndim)
    operands = (*state, *weights)
    width = steps * products
    rows = scen // NEAR
    out_shape = [jax.ShapeDtypeStruct((rows, width), jnp.float32)] * NEAR
    out_specs = [pl.BlockSpec((rows, width), lambda t: (0, 0))] * NEAR
    level_shape = (paths, factors, scen)
    scratch = [
        pltpu.VMEM((products * steps, scen), jnp.float32),
        pltpu.VMEM((scen, width), jnp.float32),
    ]
    if last:
        scratch = [pltpu.VMEM(level_shape, jnp.float32)] + scratch
    else:
        out_shape.append(jax.ShapeDtypeStruct(level_shape, jnp.float32))
        out_specs.append(pl.BlockSpec(level_shape, lambda t: (0, 0, 0)))
    return pl.pallas_call(
        functools.partial(simulate_kernel, first, last, blocks),
        grid=(blocks,),
        out_shape=out_shape,
        in_specs=[
            pl.BlockSpec(memory_space=pltpu.SMEM),
            pl.BlockSpec(
                (STEPS_PER_BLOCK, factors, paths, scen), lambda t: (t + offset, 0, 0, 0)
            ),
            *[whole(a) for a in operands],
        ],
        out_specs=out_specs,
        scratch_shapes=scratch,
        compiler_params=pltpu.CompilerParams(vmem_limit_bytes=VMEM_BYTES),
        cost_estimate=pl.CostEstimate(
            flops=steps * 500_000_000, bytes_accessed=steps * 2_000_000, transcendentals=0
        ),
        name="simulate",
    )(spot, increments, *operands)


def combine_kernel(chunks, spot_ref, *refs):
    far = lax.div(spot_ref[0], NEAR)
    parts, outs = refs[: NEAR * chunks], refs[NEAR * chunks :]
    count = len(outs) - 1
    total = outs[count]
    begin = 0
    for chunk in range(chunks):
        piece = parts[chunk * NEAR][...]
        for other in parts[chunk * NEAR + 1 : (chunk + 1) * NEAR]:
            piece = piece + other[...]
        total[:, begin : begin + piece.shape[1]] = piece
        begin += piece.shape[1]
    for across in range(count):
        spot = pl.multiple_of(jnp.bitwise_xor(far, across) * SUB, SUB)
        outs[across][...] = total[pl.ds(spot, SUB), :]


def combine(spot, parts, width):
    rows = parts[0].shape[0]
    count = rows // SUB
    return pl.pallas_call(
        functools.partial(combine_kernel, len(parts) // NEAR),
        out_shape=[jax.ShapeDtypeStruct((SUB, width), jnp.float32)] * count,
        in_specs=[pl.BlockSpec(memory_space=pltpu.SMEM)]
        + [pl.BlockSpec(memory_space=pltpu.VMEM)] * len(parts),
        scratch_shapes=[pltpu.VMEM((rows, width), jnp.float32)],
        name="combine",
    )(spot, *parts)


def finish_kernel(paths_total, *refs):
    parts, (reserve_ref, fine_ref, corr_ref) = refs[:-3], refs[-3:]
    products = reserve_ref.shape[1]
    width = parts[0].shape[1]
    half = len(parts) // 2
    mine = parts[0][...]
    theirs = parts[half][...]
    for index in range(1, half):
        mine = mine + parts[index][...]
        theirs = theirs + parts[half + index][...]
    reserve = reserve_ref[...]
    limit = jnp.concatenate([reserve] * (width // products), axis=1)
    scale = 1.0 / paths_total
    fine = jnp.maximum((mine + theirs) * scale - limit, 0.0)
    coarse = 0.5 * (
        jnp.maximum(mine * (2.0 * scale) - limit, 0.0)
        + jnp.maximum(theirs * (2.0 * scale) - limit, 0.0)
    )
    gap = fine - coarse

    def over_steps(term):
        lanes = 2 * products
        total = term[:, :lanes]
        for start in range(lanes, width, lanes):
            total = total + term[:, start : start + lanes]
        return (total[:, :products] + total[:, products:]) * (products / width)

    fine_ref[...] = over_steps(fine)
    corr_ref[...] = over_steps(gap)


def swap(value, distance, count):
    return lax.ppermute(value, "path", [(i, i ^ distance) for i in range(count)])


def per_device(
    increments,
    outer_shock,
    outer_vol,
    factor_vol,
    factor_mix,
    leg_factor,
    leg_weight,
    strike,
    reserve,
):
    product_count = strike.shape[0]
    step_count, _, paths_here, scen_rows = increments.shape
    path_count = lax.axis_size("path")
    far_count = path_count // NEAR
    paths_total = paths_here * path_count
    spot = lax.axis_index("path").astype(jnp.int32).reshape(1)

    own = outer_shock.T
    stack = jnp.stack([own] + [swap(own, d, path_count) for d in range(1, NEAR)])
    stacks = [stack] + [swap(stack, d * NEAR, path_count) for d in range(1, far_count)]

    mix_w, val_w, drift, strike_wide, scale = prepare(
        (1.0 / step_count) ** 0.5,
        scen_rows,
        outer_vol,
        factor_vol,
        factor_mix,
        leg_factor,
        leg_weight,
        strike,
    )
    weights = (mix_w, val_w, drift, strike_wide)
    parts = []
    state = (*stacks, scale)
    begin = 0
    for steps in CHUNKS:
        last = begin + steps == step_count
        made = simulate(begin, steps, last, spot, increments, state, weights)
        parts.append(made[0])
        parts.extend(swap(made[d], d, path_count) for d in range(1, NEAR))
        state = tuple(made[NEAR:])
        begin += steps
    sums = combine(spot, parts, step_count * product_count)
    pieces = [sums[0]] + [swap(sums[d], d * NEAR, path_count) for d in range(1, far_count)]
    out = jax.ShapeDtypeStruct(reserve.shape, jnp.float32)
    return pl.pallas_call(
        functools.partial(finish_kernel, paths_total), out_shape=(out, out), name="finish"
    )(*pieces, reserve)


def solution(mesh):
    in_specs = (
        P(None, None, "path", "scen"),
        P(None, ("scen", "path")),
        P(),
        P(),
        P(),
        P(),
        P(),
        P(),
        P(("scen", "path"), None),
    )
    out_specs = (P(("scen", "path"), None), P(("scen", "path"), None))
    return jax.shard_map(
        per_device, mesh=mesh, in_specs=in_specs, out_specs=out_specs, check_vma=False
    )
```

```python
import functools
import jax
import jax.numpy as jnp
from jax import lax
from jax.experimental import pallas as pl
from jax.experimental.pallas import tpu as pltpu
from jax.sharding import PartitionSpec as P

SUB = 8
NEAR = 4
STEPS_PER_BLOCK = 2
VMEM_BYTES = 50 * 1024 * 1024
SMALL_BYTES = 8 * 1024 * 1024


def split_two(full):
    high = full.astype(jnp.bfloat16)
    low = (full - high.astype(jnp.float32)).astype(jnp.bfloat16)
    return high, low


def iota(shape, dim):
    return lax.broadcasted_iota(jnp.int32, shape, dim)


def prepare_kernel(
    root_step,
    scen,
    vol_ref,
    base_ref,
    mix_ref,
    leg_ref,
    weight_ref,
    strike_ref,
    mix_out,
    val_out,
    drift_out,
    strike_out,
    scale_out,
):
    factors = mix_ref.shape[0]
    legs, products = leg_ref.shape
    same = iota((factors, factors), 0) == iota((factors, factors), 1)
    column = lambda row, pick: jnp.sum(jnp.where(pick, row, 0.0), axis=1, keepdims=True)
    half_vol = column(base_ref[...], same) * (0.5 * root_step)
    drift_out[...] = jnp.broadcast_to(0.5 * half_vol * half_vol, (factors, scen))
    scale_out[...] = jnp.broadcast_to(column(vol_ref[...], same), (factors, scen))
    square = iota((products, products), 0) == iota((products, products), 1)
    strike_out[...] = jnp.broadcast_to(column(strike_ref[...], square), (products, scen))

    high, low = split_two(half_vol * mix_ref[...])
    wide = factors * SUB
    spread = (iota((factors, wide), 0) == iota((factors, wide), 1) // SUB).astype(jnp.bfloat16)
    rows = jnp.concatenate(
        [
            jnp.dot(high, spread, preferred_element_type=jnp.float32),
            jnp.dot(low, spread, preferred_element_type=jnp.float32),
        ],
        axis=1,
    )
    lane = iota((factors, 2 * wide), 1) % SUB
    for path in range(SUB):
        mix_out[path * factors : (path + 1) * factors, :] = jnp.where(
            lane == path, rows, 0.0
        ).astype(jnp.bfloat16)

    ids = iota((factors, products), 0)
    exposure = jnp.zeros((factors, products), jnp.float32)
    for leg in range(legs):
        hit = leg_ref[leg : leg + 1, :] == ids
        exposure = exposure + jnp.where(hit, weight_ref[leg : leg + 1, :], 0.0)
    high, low = split_two(exposure)
    span = 2 * 3 * factors
    lane = iota((factors, span), 1)
    match = iota((factors, span), 0) == lane % factors
    third = (lane // factors) % 3
    put_high = jnp.logical_and(match, third != 2).astype(jnp.bfloat16)
    put_low = jnp.logical_and(match, third == 2).astype(jnp.bfloat16)
    turned = (((0,), (0,)), ((), ()))
    weights = lax.dot_general(
        high, put_high, turned, preferred_element_type=jnp.float32
    ) + lax.dot_general(low, put_low, turned, preferred_element_type=jnp.float32)
    block = iota((products, span), 1) // (3 * factors)
    for path in range(2):
        val_out[path * products : (path + 1) * products, :] = jnp.where(
            block == path, weights, 0.0
        ).astype(jnp.bfloat16)


def prepare(root_step, scen, outer_vol, factor_vol, factor_mix, leg_factor, leg_weight, strike):
    factors = factor_mix.shape[0]
    products = strike.shape[0]
    shapes = (
        ((SUB * factors, 2 * SUB * factors), jnp.bfloat16),
        ((2 * products, 6 * factors), jnp.bfloat16),
        ((factors, scen), jnp.float32),
        ((products, scen), jnp.float32),
        ((factors, scen), jnp.float32),
    )
    return pl.pallas_call(
        functools.partial(prepare_kernel, root_step, scen),
        out_shape=tuple(jax.ShapeDtypeStruct(s, d) for s, d in shapes),
        compiler_params=pltpu.CompilerParams(vmem_limit_bytes=SMALL_BYTES),
        cost_estimate=pl.CostEstimate(flops=20_000_000, bytes_accessed=1_000_000, transcendentals=0),
        name="prepare",
    )(
        outer_vol.reshape(1, factors),
        factor_vol.reshape(1, factors),
        factor_mix,
        leg_factor.T,
        leg_weight.T,
        strike.reshape(1, products),
    )


def run_steps(inc_ref, mix_ref, val_ref, drift, strike, level, sums, first_row):
    block_steps, factors, paths, scen = inc_ref.shape
    products = strike.shape[0]
    unit = 2 * SUB
    units = [(step, start) for step in range(block_steps) for start in range(0, paths, unit)]

    def shock_of(step, start):
        chunk = inc_ref[step, :, start : start + unit, :].astype(jnp.float32)
        halves = [
            chunk[:, side * SUB : (side + 1) * SUB, :].reshape(factors * SUB, scen)
            for side in range(2)
        ]
        normals = jnp.concatenate([h.astype(jnp.bfloat16) for h in halves], axis=1)
        normals = jnp.concatenate([normals, normals], axis=0)
        return jnp.dot(mix_ref[...], normals, preferred_element_type=jnp.float32)

    def grow(shock, start, path, side):
        row = path * factors
        part = shock[row : row + factors, side * scen : (side + 1) * scen]
        place = start + side * SUB + path
        old = level[place]
        wide = jnp.tanh(old) + 2.0
        new = old + wide * (part - drift * wide)
        level[place] = new
        high, low = split_two(jnp.exp(new))
        return jnp.concatenate([high, low, high], axis=0)

    def fold(acc, values):
        for path in range(2):
            for side in range(2):
                piece = values[
                    path * products : (path + 1) * products, side * scen : (side + 1) * scen
                ]
                acc = acc + jnp.maximum(piece, strike)
        return acc

    waiting = None
    acc = None
    shock = shock_of(*units[0])
    for index, (step, start) in enumerate(units):
        ahead = shock_of(*units[index + 1]) if index + 1 < len(units) else None
        for pair in range(SUB // 2):
            sides = []
            for side in range(2):
                sides.append(
                    jnp.concatenate(
                        [grow(shock, start, 2 * pair + path, side) for path in range(2)], axis=0
                    )
                )
            operand = jnp.concatenate(sides, axis=1)
            values = jnp.dot(val_ref[...], operand, preferred_element_type=jnp.float32)
            if waiting is not None:
                acc = fold(acc, waiting)
            if start == 0 and pair == 0:
                if acc is not None:
                    sums[pl.ds(first_row + (step - 1) * products, products), :] = acc
                acc = strike * (-1.0 * paths)
            waiting = values
        shock = ahead
    acc = fold(acc, waiting)
    sums[pl.ds(first_row + (block_steps - 1) * products, products), :] = acc


def simulate_kernel(
    blocks,
    inc_ref,
    begin_ref,
    scale_ref,
    mix_ref,
    val_ref,
    drift_ref,
    strike_ref,
    out_ref,
    level,
    sums,
    result,
):
    block = pl.program_id(0)
    block_steps, factors, paths, scen = inc_ref.shape
    products = strike_ref.shape[0]
    far = out_ref.shape[1] // SUB

    @pl.when(block == 0)
    def _():
        begin = jnp.transpose(begin_ref[...])[0:factors, :] * scale_ref[...]
        for path in range(paths):
            level[path] = begin

    run_steps(
        inc_ref,
        mix_ref,
        val_ref,
        drift_ref[...],
        strike_ref[...],
        level,
        sums,
        pl.multiple_of(block * block_steps * products, products),
    )

    @pl.when(block == blocks - 1)
    def _():
        result[...] = jnp.transpose(sums[...])
        for near in range(NEAR):
            for place in range(far):
                begin = (place * NEAR + near) * SUB
                out_ref[near, place * SUB : (place + 1) * SUB, :] = result[begin : begin + SUB, :]


def simulate(increments, begin, scale, mix_w, val_w, drift, strike):
    steps, factors, paths, scen = increments.shape
    products = strike.shape[0]
    blocks = steps // STEPS_PER_BLOCK
    whole = lambda shape: pl.BlockSpec(shape, lambda t: (0,) * len(shape))
    operands = (begin, scale, mix_w, val_w, drift, strike)
    width = steps * products
    shape = (NEAR, scen // NEAR, width)
    return pl.pallas_call(
        functools.partial(simulate_kernel, blocks),
        grid=(blocks,),
        out_shape=jax.ShapeDtypeStruct(shape, jnp.float32),
        in_specs=[
            pl.BlockSpec((STEPS_PER_BLOCK, factors, paths, scen), lambda t: (t, 0, 0, 0)),
            *[whole(a.shape) for a in operands],
        ],
        out_specs=whole(shape),
        scratch_shapes=[
            pltpu.VMEM((paths, factors, scen), jnp.float32),
            pltpu.VMEM((width, scen), jnp.float32),
            pltpu.VMEM((scen, width), jnp.float32),
        ],
        compiler_params=pltpu.CompilerParams(vmem_limit_bytes=VMEM_BYTES),
        cost_estimate=pl.CostEstimate(
            flops=steps * 500_000_000, bytes_accessed=steps * 2_000_000, transcendentals=0
        ),
        name="simulate",
    )(increments, *operands)


def combine_kernel(parts_ref, out_ref):
    count = parts_ref.shape[0]
    for place in range(out_ref.shape[0]):
        rows = pl.ds(place * SUB, SUB)
        total = parts_ref[0, rows, :]
        for index in range(1, count):
            total = total + parts_ref[index, rows, :]
        out_ref[place] = total


def combine(parts):
    _, rows, width = parts.shape
    return pl.pallas_call(
        combine_kernel,
        out_shape=jax.ShapeDtypeStruct((rows // SUB, SUB, width), jnp.float32),
        compiler_params=pltpu.CompilerParams(vmem_limit_bytes=SMALL_BYTES),
        name="combine",
    )(parts)


def finish_kernel(paths_total, parts_ref, reserve_ref, fine_ref, corr_ref):
    products = reserve_ref.shape[1]
    count, _, width = parts_ref.shape
    half = count // 2
    first = parts_ref[0]
    second = parts_ref[half]
    for index in range(1, half):
        first = first + parts_ref[index]
        second = second + parts_ref[half + index]
    reserve = reserve_ref[...]
    limit = jnp.concatenate([reserve] * (width // products), axis=1)
    scale = 1.0 / paths_total
    fine = jnp.maximum((first + second) * scale - limit, 0.0)
    coarse = 0.5 * (
        jnp.maximum(first * (2.0 * scale) - limit, 0.0)
        + jnp.maximum(second * (2.0 * scale) - limit, 0.0)
    )
    gap = fine - coarse

    def over_steps(term):
        lanes = 2 * products
        total = term[:, :lanes]
        for start in range(lanes, width, lanes):
            total = total + term[:, start : start + lanes]
        return (total[:, :products] + total[:, products:]) * (products / width)

    fine_ref[...] = over_steps(fine)
    corr_ref[...] = over_steps(gap)


def per_device(
    increments,
    outer_shock,
    outer_vol,
    factor_vol,
    factor_mix,
    leg_factor,
    leg_weight,
    strike,
    reserve,
):
    step_count, factors, paths_here, scen_rows = increments.shape
    path_count = lax.axis_size("path")
    far_count = path_count // NEAR
    paths_total = paths_here * path_count
    near_groups = [[f * NEAR + n for n in range(NEAR)] for f in range(far_count)]
    far_groups = [[f * NEAR + n for f in range(far_count)] for n in range(NEAR)]

    def exchange(blocks, groups):
        return lax.all_to_all(blocks, "path", 0, 0, axis_index_groups=groups, tiled=True)

    def spread(block, count):
        return jnp.broadcast_to(block[None], (count, *block.shape))

    own = jnp.pad(outer_shock.T, ((0, 0), (0, scen_rows - factors)))
    near_rows = exchange(spread(own, NEAR), near_groups)
    near_rows = near_rows.reshape(NEAR * own.shape[0], scen_rows)
    begin = exchange(spread(near_rows, far_count), far_groups).reshape(scen_rows, scen_rows)

    mix_w, val_w, drift, strike_wide, scale = prepare(
        (1.0 / step_count) ** 0.5,
        scen_rows,
        outer_vol,
        factor_vol,
        factor_mix,
        leg_factor,
        leg_weight,
        strike,
    )
    local = simulate(increments, begin, scale, mix_w, val_w, drift, strike_wide)
    parts = exchange(combine(exchange(local, near_groups)), far_groups)
    out = jax.ShapeDtypeStruct(reserve.shape, jnp.float32)
    return pl.pallas_call(
        functools.partial(finish_kernel, paths_total),
        out_shape=(out, out),
        compiler_params=pltpu.CompilerParams(vmem_limit_bytes=SMALL_BYTES),
        name="finish",
    )(parts, reserve)


def solution(mesh):
    in_specs = (
        P(None, None, "path", "scen"),
        P(None, ("scen", "path")),
        P(),
        P(),
        P(),
        P(),
        P(),
        P(),
        P(("scen", "path"), None),
    )
    out_specs = (P(("scen", "path"), None), P(("scen", "path"), None))
    return jax.shard_map(
        per_device, mesh=mesh, in_specs=in_specs, out_specs=out_specs, check_vma=False
    )
```

```python
import functools
import jax
import jax.numpy as jnp
from jax import lax
from jax.experimental import pallas as pl
from jax.experimental.pallas import tpu as pltpu
from jax.sharding import PartitionSpec as P

SUB = 8
NEAR = 4
STEPS_PER_TURN = 4
SHOCK_BYTES = 37 * 1024 * 1024
SMALL_BYTES = 8 * 1024 * 1024


def split_two(full):
    high = full.astype(jnp.bfloat16)
    low = (full - high.astype(jnp.float32)).astype(jnp.bfloat16)
    return high, low


def iota(shape, dim):
    return lax.broadcasted_iota(jnp.int32, shape, dim)


def prepare_kernel(
    root_step, products, pack_ref, rows_out, vol_out, val_out, drift_out, strike_out
):
    factors = rows_out.shape[0]
    scen = drift_out.shape[1]
    legs = (pack_ref.shape[0] - factors - SUB) // 2
    mix = pack_ref[0:factors, 0:factors]
    leg_factor = pack_ref[factors : factors + legs, 0:products]
    leg_weight = pack_ref[factors + legs : factors + 2 * legs, 0:products]
    tail = factors + 2 * legs
    vol_out[...] = jnp.broadcast_to(pack_ref[tail : tail + 1, :], vol_out.shape)
    base = pack_ref[tail + 1 : tail + 2, 0:factors]
    strike = pack_ref[tail + 2 : tail + 3, 0:products]
    column = lambda row, pick: jnp.sum(jnp.where(pick, row, 0.0), axis=1, keepdims=True)
    same = iota((factors, factors), 0) == iota((factors, factors), 1)
    half_vol = column(base, same) * (0.5 * root_step)
    drift_out[...] = jnp.broadcast_to(0.5 * half_vol * half_vol, (factors, scen))
    square = iota((products, products), 0) == iota((products, products), 1)
    strike_out[...] = jnp.broadcast_to(column(strike, square), (products, scen))

    high, low = split_two(half_vol * mix)
    wide = factors * SUB
    spread = (iota((factors, wide), 0) == iota((factors, wide), 1) // SUB).astype(jnp.bfloat16)
    rows_out[:, 0:wide] = jnp.dot(high, spread, preferred_element_type=jnp.float32)
    rows_out[:, wide:] = jnp.dot(low, spread, preferred_element_type=jnp.float32)

    ids = iota((factors, products), 0).astype(jnp.float32)
    exposure = jnp.zeros((factors, products), jnp.float32)
    for leg in range(legs):
        hit = leg_factor[leg : leg + 1, :] == ids
        exposure = exposure + jnp.where(hit, leg_weight[leg : leg + 1, :], 0.0)
    high, low = split_two(exposure)
    span = 2 * 3 * factors
    lane = iota((factors, span), 1)
    match = iota((factors, span), 0) == lane % factors
    third = (lane // factors) % 3
    put_high = jnp.logical_and(match, third != 2).astype(jnp.bfloat16)
    put_low = jnp.logical_and(match, third == 2).astype(jnp.bfloat16)
    turned = (((0,), (0,)), ((), ()))
    weights = lax.dot_general(
        high, put_high, turned, preferred_element_type=jnp.float32
    ) + lax.dot_general(low, put_low, turned, preferred_element_type=jnp.float32)
    block = iota((products, span), 1) // (3 * factors)
    for path in range(2):
        val_out[path * products : (path + 1) * products, :] = jnp.where(
            block == path, weights, 0.0
        ).astype(jnp.bfloat16)


def prepare(steps, scen, outer_vol, factor_vol, factor_mix, leg_factor, leg_weight, strike):
    factors = factor_mix.shape[0]
    products = strike.shape[0]

    legs = leg_factor.shape[1]
    height = factors + 2 * legs + SUB
    pack = jnp.zeros((height, scen), jnp.float32)
    start = 0
    for part in (
        factor_mix,
        leg_factor.T.astype(jnp.float32),
        leg_weight.T,
        outer_vol[None],
        factor_vol[None],
        strike[None],
    ):
        count, width = part.shape
        edges = ((start, height - start - count, 0), (0, scen - width, 0))
        pack = pack + lax.pad(part, jnp.float32(0.0), edges)
        start += count
    shapes = (
        ((factors, 2 * SUB * factors), jnp.float32),
        ((SUB, scen), jnp.float32),
        ((2 * products, 6 * factors), jnp.bfloat16),
        ((factors, scen), jnp.float32),
        ((products, scen), jnp.float32),
    )
    return pl.pallas_call(
        functools.partial(prepare_kernel, (1.0 / steps) ** 0.5, products),
        out_shape=tuple(pltpu.VMEM(s, d) for s, d in shapes),
        compiler_params=pltpu.CompilerParams(vmem_limit_bytes=SMALL_BYTES),
        cost_estimate=pl.CostEstimate(flops=500_000_000, bytes_accessed=500_000, transcendentals=0),
        name="prepare",
    )(pack)


def relay_kernel(near_ref, vol_ref, rows_ref, begin_out, mix_out):
    factors, wide = rows_ref.shape
    lane = iota((factors, wide), 1) % SUB
    rows = rows_ref[...]
    begin = near_ref[...] * vol_ref[0:1, :]
    for place in range(begin_out.shape[0]):
        begin_out[place] = begin
    for path in range(SUB):
        mix_out[path * factors : (path + 1) * factors, :] = jnp.where(
            lane == path, rows, 0.0
        ).astype(jnp.bfloat16)


def relay(far_count, near_rows, vol, rows):
    factors, wide = rows.shape
    return pl.pallas_call(
        relay_kernel,
        out_shape=(
            pltpu.VMEM((far_count, *near_rows.shape), jnp.float32),
            pltpu.VMEM((SUB * factors, wide), jnp.bfloat16),
        ),
        compiler_params=pltpu.CompilerParams(vmem_limit_bytes=SMALL_BYTES),
        name="relay",
    )(near_rows, vol, rows)


def shocks_kernel(inc_hbm, mix_ref, shock_out, inc, arrived):
    steps, factors, paths, scen = inc.shape
    unit = 2 * SUB
    units = paths // unit

    def fetch(step):
        return pltpu.make_async_copy(inc_hbm.at[step], inc.at[step], arrived.at[step])

    for step in range(steps):
        fetch(step).start()

    def turn(index, carry):
        for inner in range(2):
            step = index * 2 + inner
            fetch(step).wait()
            for place in range(units):
                chunk = inc[step, :, place * unit : (place + 1) * unit, :].astype(jnp.float32)
                sides = [
                    chunk[:, side * SUB : (side + 1) * SUB, :].reshape(factors * SUB, scen)
                    for side in range(2)
                ]
                normals = jnp.concatenate([x.astype(jnp.bfloat16) for x in sides], axis=1)
                normals = jnp.concatenate([normals, normals], axis=0)
                shock_out[step * units + place] = jnp.dot(
                    mix_ref[...], normals, preferred_element_type=jnp.float32
                )
        return carry

    lax.fori_loop(0, steps // 2, turn, 0)


def shocks(increments, mix_w):
    steps, factors, paths, scen = increments.shape
    rows = SUB * factors
    units = paths // (2 * SUB)
    vmem = pl.BlockSpec(memory_space=pltpu.VMEM)
    return pl.pallas_call(
        shocks_kernel,
        out_shape=pltpu.VMEM((steps * units, rows, 2 * scen), jnp.float32),
        in_specs=[pl.BlockSpec(memory_space=pl.ANY), vmem],
        out_specs=vmem,
        scratch_shapes=[
            pltpu.VMEM(increments.shape, increments.dtype),
            pltpu.SemaphoreType.DMA((steps,)),
        ],
        compiler_params=pltpu.CompilerParams(vmem_limit_bytes=SHOCK_BYTES),
        cost_estimate=pl.CostEstimate(
            flops=5_000_000_000, bytes_accessed=8_400_000, transcendentals=0
        ),
        name="shocks",
    )(increments, mix_w)


def simulate_kernel(
    begin_ref, shock_ref, val_ref, drift_ref, strike_ref, out_ref, level, sums
):
    paths, factors, scen = level.shape
    products = strike_ref.shape[0]
    unit = 2 * SUB
    units = paths // unit
    steps = shock_ref.shape[0] // units
    far = out_ref.shape[1] // SUB
    turns = steps // STEPS_PER_TURN
    wide_turn = STEPS_PER_TURN * products
    drift = drift_ref[...]
    strike = strike_ref[...]

    begin = jnp.transpose(begin_ref[...])[0:factors, :]
    for path in range(paths):
        level[path] = begin

    def grow(index, place, path, side):
        row = path * factors
        part = shock_ref[index, row : row + factors, side * scen : (side + 1) * scen]
        spot = place * unit + side * SUB + path
        old = level[spot]
        wide = jnp.tanh(old) + 2.0
        new = old + wide * (part - drift * wide)
        level[spot] = new
        high, low = split_two(jnp.exp(new))
        return jnp.concatenate([high, low, high], axis=0)

    def fold(acc, values):
        for path in range(2):
            for side in range(2):
                piece = values[
                    path * products : (path + 1) * products, side * scen : (side + 1) * scen
                ]
                acc = acc + jnp.maximum(piece, strike)
        return acc

    def send(turn):
        turned = jnp.transpose(sums[...])
        cols = pl.ds(pl.multiple_of(turn * wide_turn, wide_turn), wide_turn)
        for near in range(NEAR):
            for place in range(far):
                first = (place * NEAR + near) * SUB
                out_ref[near, place * SUB : (place + 1) * SUB, cols] = turned[
                    first : first + SUB, :
                ]

    def run(turn, carry):
        send(jnp.maximum(turn - 1, 0))
        waiting = None
        acc = None
        for inner in range(STEPS_PER_TURN):
            for place in range(units):
                index = (turn * STEPS_PER_TURN + inner) * units + place
                for pair in range(SUB // 2):
                    sides = []
                    for side in range(2):
                        sides.append(
                            jnp.concatenate(
                                [grow(index, place, 2 * pair + path, side) for path in range(2)],
                                axis=0,
                            )
                        )
                    operand = jnp.concatenate(sides, axis=1)
                    values = jnp.dot(val_ref[...], operand, preferred_element_type=jnp.float32)
                    if waiting is not None:
                        acc = fold(acc, waiting)
                    if place == 0 and pair == 0:
                        if acc is not None:
                            sums[(inner - 1) * products : inner * products, :] = acc
                        acc = strike * (-1.0 * paths)
                    waiting = values
        sums[wide_turn - products :, :] = fold(acc, waiting)
        return carry

    sums[...] = jnp.zeros_like(sums)
    lax.fori_loop(0, turns, run, 0)
    send(turns - 1)


def simulate(paths, begin, shock, val_w, drift, strike):
    factors, scen = drift.shape
    products = strike.shape[0]
    steps = shock.shape[0] // (paths // (2 * SUB))
    vmem = pl.BlockSpec(memory_space=pltpu.VMEM)
    return pl.pallas_call(
        simulate_kernel,
        out_shape=jax.ShapeDtypeStruct((NEAR, scen // NEAR, steps * products), jnp.float32),
        in_specs=[vmem] * 5,
        out_specs=vmem,
        scratch_shapes=[
            pltpu.VMEM((paths, factors, scen), jnp.float32),
            pltpu.VMEM((STEPS_PER_TURN * products, scen), jnp.float32),
        ],
        compiler_params=pltpu.CompilerParams(vmem_limit_bytes=SMALL_BYTES),
        cost_estimate=pl.CostEstimate(
            flops=10_000_000_000, bytes_accessed=1_000_000, transcendentals=0
        ),
        name="simulate",
    )(begin, shock, val_w, drift, strike)


def combine_kernel(parts_ref, out_ref):
    count = parts_ref.shape[0]
    for place in range(out_ref.shape[0]):
        rows = pl.ds(place * SUB, SUB)
        total = parts_ref[0, rows, :]
        for index in range(1, count):
            total = total + parts_ref[index, rows, :]
        out_ref[place] = total


def combine(parts):
    _, rows, width = parts.shape
    return pl.pallas_call(
        combine_kernel,
        out_shape=jax.ShapeDtypeStruct((rows // SUB, SUB, width), jnp.float32),
        compiler_params=pltpu.CompilerParams(vmem_limit_bytes=SMALL_BYTES),
        name="combine",
    )(parts)


def finish_kernel(paths_total, parts_ref, reserve_ref, fine_ref, corr_ref):
    products = reserve_ref.shape[1]
    count, _, width = parts_ref.shape
    half = count // 2
    first = parts_ref[0]
    second = parts_ref[half]
    for index in range(1, half):
        first = first + parts_ref[index]
        second = second + parts_ref[half + index]
    reserve = reserve_ref[...]
    limit = jnp.concatenate([reserve] * (width // products), axis=1)
    scale = 1.0 / paths_total
    fine = jnp.maximum((first + second) * scale - limit, 0.0)
    coarse = 0.5 * (
        jnp.maximum(first * (2.0 * scale) - limit, 0.0)
        + jnp.maximum(second * (2.0 * scale) - limit, 0.0)
    )
    gap = fine - coarse

    def over_steps(term):
        lanes = 2 * products
        total = term[:, :lanes]
        for start in range(lanes, width, lanes):
            total = total + term[:, start : start + lanes]
        return (total[:, :products] + total[:, products:]) * (products / width)

    fine_ref[...] = over_steps(fine)
    corr_ref[...] = over_steps(gap)


def per_device(
    increments,
    outer_shock,
    outer_vol,
    factor_vol,
    factor_mix,
    leg_factor,
    leg_weight,
    strike,
    reserve,
):
    step_count, factors, paths_here, scen_rows = increments.shape
    path_count = lax.axis_size("path")
    far_count = path_count // NEAR
    paths_total = paths_here * path_count
    near_groups = [[f * NEAR + n for n in range(NEAR)] for f in range(far_count)]
    far_groups = [[f * NEAR + n for f in range(far_count)] for n in range(NEAR)]

    def exchange(blocks, groups):
        return lax.all_to_all(blocks, "path", 0, 0, axis_index_groups=groups, tiled=True)

    own = jnp.pad(outer_shock.T, ((0, 0), (0, scen_rows - factors)))
    near_rows = exchange(jnp.broadcast_to(own[None], (NEAR, *own.shape)), near_groups)
    rows, vol, val_w, drift, strike_wide = prepare(
        step_count, scen_rows, outer_vol, factor_vol, factor_mix, leg_factor, leg_weight, strike
    )
    blocks, mix_w = relay(far_count, near_rows.reshape(-1, scen_rows), vol, rows)
    begin = exchange(blocks, far_groups).reshape(scen_rows, scen_rows)
    shock = shocks(increments, mix_w)
    local = simulate(paths_here, begin, shock, val_w, drift, strike_wide)
    parts = exchange(combine(exchange(local, near_groups)), far_groups)
    out = jax.ShapeDtypeStruct(reserve.shape, jnp.float32)
    return pl.pallas_call(
        functools.partial(finish_kernel, paths_total),
        out_shape=(out, out),
        compiler_params=pltpu.CompilerParams(vmem_limit_bytes=SMALL_BYTES),
        name="finish",
    )(parts, reserve)


def solution(mesh):
    in_specs = (
        P(None, None, "path", "scen"),
        P(None, ("scen", "path")),
        P(),
        P(),
        P(),
        P(),
        P(),
        P(),
        P(("scen", "path"), None),
    )
    out_specs = (P(("scen", "path"), None), P(("scen", "path"), None))
    return jax.shard_map(
        per_device, mesh=mesh, in_specs=in_specs, out_specs=out_specs, check_vma=False
    )
```

```python
import functools
import jax
import jax.numpy as jnp
from jax import lax
from jax.experimental import pallas as pl
from jax.experimental.pallas import tpu as pltpu
from jax.sharding import PartitionSpec as P

SUB = 8
NEAR = 4
TURNS = (0, 2, 1, 3)
ARRIVE = (0, 3, 1, 2)
STEPS_PER_BLOCK = 4
VMEM_BYTES = 50 * 1024 * 1024
SMALL_BYTES = 8 * 1024 * 1024


def split_two(full):
    high = full.astype(jnp.bfloat16)
    low = (full - high.astype(jnp.float32)).astype(jnp.bfloat16)
    return high, low


def iota(shape, dim):
    return lax.broadcasted_iota(jnp.int32, shape, dim)


def prepare_kernel(
    root_step, products, pack_ref, mix_out, own_out, vol_out, val_out, drift_out, strike_out
):
    factors = mix_out.shape[0] // SUB
    scen = drift_out.shape[1]
    legs = (pack_ref.shape[0] - factors - 2 * SUB) // 2
    mix = pack_ref[0:factors, 0:factors]
    leg_factor = pack_ref[factors : factors + legs, 0:products]
    leg_weight = pack_ref[factors + legs : factors + 2 * legs, 0:products]
    own = factors + 2 * legs
    own_out[...] = pack_ref[own : own + SUB, :]
    tail = own + SUB
    vol_out[...] = jnp.broadcast_to(pack_ref[tail : tail + 1, :], vol_out.shape)
    base = pack_ref[tail + 1 : tail + 2, 0:factors]
    strike = pack_ref[tail + 2 : tail + 3, 0:products]
    column = lambda row, pick: jnp.sum(jnp.where(pick, row, 0.0), axis=1, keepdims=True)
    same = iota((factors, factors), 0) == iota((factors, factors), 1)
    half_vol = column(base, same) * (0.5 * root_step)
    drift_out[...] = jnp.broadcast_to(0.5 * half_vol * half_vol, (factors, scen))
    square = iota((products, products), 0) == iota((products, products), 1)
    strike_out[...] = jnp.broadcast_to(column(strike, square), (products, scen))

    high, low = split_two(half_vol * mix)
    wide = factors * SUB
    spread = (iota((factors, wide), 0) == iota((factors, wide), 1) // SUB).astype(jnp.bfloat16)
    rows = jnp.concatenate(
        [
            jnp.dot(high, spread, preferred_element_type=jnp.float32),
            jnp.dot(low, spread, preferred_element_type=jnp.float32),
        ],
        axis=1,
    )
    lane = iota((factors, 2 * wide), 1) % SUB
    for path in range(SUB):
        mix_out[path * factors : (path + 1) * factors, :] = jnp.where(
            lane == path, rows, 0.0
        ).astype(jnp.bfloat16)

    ids = iota((factors, products), 0).astype(jnp.float32)
    exposure = jnp.zeros((factors, products), jnp.float32)
    for leg in range(legs):
        hit = leg_factor[leg : leg + 1, :] == ids
        exposure = exposure + jnp.where(hit, leg_weight[leg : leg + 1, :], 0.0)
    high, low = split_two(exposure)
    span = 2 * 3 * factors
    lane = iota((factors, span), 1)
    match = iota((factors, span), 0) == lane % factors
    third = (lane // factors) % 3
    put_high = jnp.logical_and(match, third != 2).astype(jnp.bfloat16)
    put_low = jnp.logical_and(match, third == 2).astype(jnp.bfloat16)
    turned = (((0,), (0,)), ((), ()))
    weights = lax.dot_general(
        high, put_high, turned, preferred_element_type=jnp.float32
    ) + lax.dot_general(low, put_low, turned, preferred_element_type=jnp.float32)
    block = iota((products, span), 1) // (3 * factors)
    for path in range(2):
        val_out[path * products : (path + 1) * products, :] = jnp.where(
            block == path, weights, 0.0
        ).astype(jnp.bfloat16)


def prepare(steps, scen, own, outer_vol, factor_vol, factor_mix, leg_factor, leg_weight, strike):
    factors = factor_mix.shape[0]
    products = strike.shape[0]

    legs = leg_factor.shape[1]
    height = factors + 2 * legs + 2 * SUB
    pack = jnp.zeros((height, scen), jnp.float32)
    start = 0
    for part in (
        factor_mix,
        leg_factor.T.astype(jnp.float32),
        leg_weight.T,
        own,
        outer_vol[None],
        factor_vol[None],
        strike[None],
    ):
        count, width = part.shape
        edges = ((start, height - start - count, 0), (0, scen - width, 0))
        pack = pack + lax.pad(part, jnp.float32(0.0), edges)
        start += count
    shapes = (
        ((SUB * factors, 2 * SUB * factors), jnp.bfloat16),
        ((SUB, scen), jnp.float32),
        ((SUB, scen), jnp.float32),
        ((2 * products, 6 * factors), jnp.bfloat16),
        ((factors, scen), jnp.float32),
        ((products, scen), jnp.float32),
    )
    return pl.pallas_call(
        functools.partial(prepare_kernel, (1.0 / steps) ** 0.5, products),
        out_shape=tuple(pltpu.VMEM(s, d) for s, d in shapes),
        compiler_params=pltpu.CompilerParams(vmem_limit_bytes=SMALL_BYTES),
        cost_estimate=pl.CostEstimate(flops=500_000_000, bytes_accessed=500_000, transcendentals=0),
        name="prepare",
    )(pack)


def relay_kernel(spot_ref, vol_ref, *refs):
    near_refs, out_ref = refs[:-1], refs[-1]
    near = lax.rem(spot_ref[0], NEAR)
    factors = near_refs[1].shape[1]
    vol = vol_ref[0:1, 0:factors]
    out_ref[...] = jnp.zeros_like(out_ref)
    for turn, near_ref in zip(ARRIVE, near_refs):
        begin = pl.multiple_of(jnp.bitwise_xor(near, turn) * SUB, SUB)
        out_ref[pl.ds(begin, SUB), 0:factors] = near_ref[:, 0:factors] * vol


def relay(spot, vol, blocks):
    vmem = pl.BlockSpec(memory_space=pltpu.VMEM)
    return pl.pallas_call(
        relay_kernel,
        out_shape=jax.ShapeDtypeStruct((NEAR * SUB, vol.shape[1]), jnp.float32),
        in_specs=[pl.BlockSpec(memory_space=pltpu.SMEM)] + [vmem] * (1 + len(blocks)),
        out_specs=vmem,
        compiler_params=pltpu.CompilerParams(vmem_limit_bytes=SMALL_BYTES),
        name="relay",
    )(spot, vol, *blocks)


def run_steps(inc_ref, mix_ref, val_ref, drift, strike, level, sums, first_row):
    block_steps, factors, paths, scen = inc_ref.shape
    products = strike.shape[0]
    unit = 2 * SUB
    units = [(step, start) for step in range(block_steps) for start in range(0, paths, unit)]

    def shock_of(step, start):
        chunk = inc_ref[step, :, start : start + unit, :].astype(jnp.float32)
        halves = [
            chunk[:, side * SUB : (side + 1) * SUB, :].reshape(factors * SUB, scen)
            for side in range(2)
        ]
        normals = jnp.concatenate([h.astype(jnp.bfloat16) for h in halves], axis=1)
        normals = jnp.concatenate([normals, normals], axis=0)
        return jnp.dot(mix_ref[...], normals, preferred_element_type=jnp.float32)

    def grow(shock, start, path, side):
        row = path * factors
        part = shock[row : row + factors, side * scen : (side + 1) * scen]
        place = start + side * SUB + path
        old = level[place]
        wide = jnp.tanh(old) + 2.0
        new = old + wide * (part - drift * wide)
        level[place] = new
        high, low = split_two(jnp.exp(new))
        return jnp.concatenate([high, low, high], axis=0)

    def fold(acc, values):
        for path in range(2):
            for side in range(2):
                piece = values[
                    path * products : (path + 1) * products, side * scen : (side + 1) * scen
                ]
                acc = acc + jnp.maximum(piece, strike)
        return acc

    waiting = None
    acc = None
    shock = shock_of(*units[0])
    for index, (step, start) in enumerate(units):
        ahead = shock_of(*units[index + 1]) if index + 1 < len(units) else None
        for pair in range(SUB // 2):
            sides = []
            for side in range(2):
                sides.append(
                    jnp.concatenate(
                        [grow(shock, start, 2 * pair + path, side) for path in range(2)], axis=0
                    )
                )
            operand = jnp.concatenate(sides, axis=1)
            values = jnp.dot(val_ref[...], operand, preferred_element_type=jnp.float32)
            if waiting is not None:
                acc = fold(acc, waiting)
            if start == 0 and pair == 0:
                if acc is not None:
                    sums[pl.ds(first_row + (step - 1) * products, products), :] = acc
                acc = strike * (-1.0 * paths)
            waiting = values
        shock = ahead
    acc = fold(acc, waiting)
    sums[pl.ds(first_row + (block_steps - 1) * products, products), :] = acc


def simulate_kernel(blocks, spot_ref, inc_ref, *refs):
    stacks, refs = refs[: len(TURNS)], refs[len(TURNS) :]
    mix_ref, val_ref, drift_ref, strike_ref = refs[:4]
    out_refs, (level, sums, result) = refs[4 : 4 + len(TURNS)], refs[4 + len(TURNS) :]
    block = pl.program_id(0)
    block_steps, _, paths, scen = inc_ref.shape
    products = strike_ref.shape[0]
    factors = level.shape[1]
    near = lax.rem(spot_ref[0], NEAR)
    far = lax.div(spot_ref[0], NEAR)

    @pl.when(block == 0)
    def _():
        rows = NEAR * SUB
        for turn, stack in zip(ARRIVE, stacks):
            start = pl.multiple_of(jnp.bitwise_xor(far, turn) * rows, rows)
            result[pl.ds(start, rows), 0:scen] = stack[...]
        begin = jnp.transpose(result[:, 0:scen])[0:factors, :]
        for path in range(paths):
            level[path] = begin

    run_steps(
        inc_ref,
        mix_ref,
        val_ref,
        drift_ref[...],
        strike_ref[...],
        level,
        sums,
        pl.multiple_of(block * block_steps * products, products),
    )

    @pl.when(block == blocks - 1)
    def _():
        result[...] = jnp.transpose(sums[...])
        for turn, out_ref in zip(TURNS, out_refs):
            other = jnp.bitwise_xor(near, turn)
            for place in range(out_ref.shape[0] // SUB):
                start = pl.multiple_of((place * NEAR + other) * SUB, SUB)
                out_ref[place * SUB : (place + 1) * SUB, :] = result[pl.ds(start, SUB), :]


def simulate(spot, increments, stacks, weights):
    steps, factors, paths, scen = increments.shape
    products = weights[3].shape[0]
    blocks = steps // STEPS_PER_BLOCK
    whole = lambda shape: pl.BlockSpec(shape, lambda t: (0,) * len(shape))
    operands = (*stacks, *weights)
    width = steps * products
    shape = (scen // NEAR, width)
    return pl.pallas_call(
        functools.partial(simulate_kernel, blocks),
        grid=(blocks,),
        out_shape=[jax.ShapeDtypeStruct(shape, jnp.float32)] * len(TURNS),
        in_specs=[
            pl.BlockSpec(memory_space=pltpu.SMEM),
            pl.BlockSpec((STEPS_PER_BLOCK, factors, paths, scen), lambda t: (t, 0, 0, 0)),
            *[whole(a.shape) for a in operands],
        ],
        out_specs=[whole(shape)] * len(TURNS),
        scratch_shapes=[
            pltpu.VMEM((paths, factors, scen), jnp.float32),
            pltpu.VMEM((width, scen), jnp.float32),
            pltpu.VMEM((scen, width), jnp.float32),
        ],
        compiler_params=pltpu.CompilerParams(vmem_limit_bytes=VMEM_BYTES),
        cost_estimate=pl.CostEstimate(
            flops=steps * 500_000_000, bytes_accessed=steps * 2_000_000, transcendentals=0
        ),
        name="simulate",
    )(spot, increments, *operands)


def combine_kernel(spot_ref, *refs):
    parts, outs = refs[: len(TURNS)], refs[len(TURNS) :]
    far = lax.div(spot_ref[0], NEAR)
    for turn, out_ref in zip(TURNS, outs):
        rows = pl.ds(pl.multiple_of(jnp.bitwise_xor(far, turn) * SUB, SUB), SUB)
        total = parts[0][rows, :]
        for part in parts[1:]:
            total = total + part[rows, :]
        out_ref[...] = total


def combine(spot, parts):
    width = parts[0].shape[1]
    vmem = pl.BlockSpec(memory_space=pltpu.VMEM)
    return pl.pallas_call(
        combine_kernel,
        out_shape=[jax.ShapeDtypeStruct((SUB, width), jnp.float32)] * len(TURNS),
        in_specs=[pl.BlockSpec(memory_space=pltpu.SMEM)] + [vmem] * len(TURNS),
        out_specs=[vmem] * len(TURNS),
        compiler_params=pltpu.CompilerParams(vmem_limit_bytes=SMALL_BYTES),
        name="combine",
    )(spot, *parts)


def finish_kernel(paths_total, *refs):
    parts, (reserve_ref, fine_ref, corr_ref) = refs[:-3], refs[-3:]
    products = reserve_ref.shape[1]
    width = parts[0].shape[1]
    half = len(parts) // 2
    mine, theirs = None, None
    for turn, part in zip(TURNS, parts):
        if turn < half:
            mine = part[...] if mine is None else mine + part[...]
        else:
            theirs = part[...] if theirs is None else theirs + part[...]
    reserve = reserve_ref[...]
    limit = jnp.concatenate([reserve] * (width // products), axis=1)
    scale = 1.0 / paths_total
    fine = jnp.maximum((mine + theirs) * scale - limit, 0.0)
    coarse = 0.5 * (
        jnp.maximum(mine * (2.0 * scale) - limit, 0.0)
        + jnp.maximum(theirs * (2.0 * scale) - limit, 0.0)
    )
    gap = fine - coarse

    def over_steps(term):
        lanes = 2 * products
        total = term[:, :lanes]
        for start in range(lanes, width, lanes):
            total = total + term[:, start : start + lanes]
        return (total[:, :products] + total[:, products:]) * (products / width)

    fine_ref[...] = over_steps(fine)
    corr_ref[...] = over_steps(gap)


def per_device(
    increments,
    outer_shock,
    outer_vol,
    factor_vol,
    factor_mix,
    leg_factor,
    leg_weight,
    strike,
    reserve,
):
    step_count, _, paths_here, scen_rows = increments.shape
    path_count = lax.axis_size("path")
    paths_total = paths_here * path_count
    spot = lax.axis_index("path").astype(jnp.int32).reshape(1)

    def swap(value, distance):
        if distance == 0:
            return value
        return lax.ppermute(value, "path", [(i, i ^ distance) for i in range(path_count)])

    own = outer_shock.T
    shared = {turn: swap(own, turn) for turn in ARRIVE}
    mix_w, shared[0], vol, val_w, drift, strike_wide = prepare(
        step_count, scen_rows, own, outer_vol, factor_vol, factor_mix, leg_factor, leg_weight, strike
    )
    rows = relay(spot, vol, [shared[turn] for turn in ARRIVE])
    stacks = [swap(rows, turn * NEAR) for turn in ARRIVE]
    local = simulate(spot, increments, stacks, (mix_w, val_w, drift, strike_wide))
    parts = [swap(value, turn) for value, turn in zip(local, TURNS)]
    sums = combine(spot, parts)
    pieces = [swap(value, turn * NEAR) for value, turn in zip(sums, TURNS)]
    out = jax.ShapeDtypeStruct(reserve.shape, jnp.float32)
    return pl.pallas_call(
        functools.partial(finish_kernel, paths_total),
        out_shape=(out, out),
        compiler_params=pltpu.CompilerParams(vmem_limit_bytes=SMALL_BYTES),
        name="finish",
    )(*pieces, reserve)


def solution(mesh):
    in_specs = (
        P(None, None, "path", "scen"),
        P(None, ("scen", "path")),
        P(),
        P(),
        P(),
        P(),
        P(),
        P(),
        P(("scen", "path"), None),
    )
    out_specs = (P(("scen", "path"), None), P(("scen", "path"), None))
    return jax.shard_map(
        per_device, mesh=mesh, in_specs=in_specs, out_specs=out_specs, check_vma=False
    )
```

```python
import functools
import jax
import jax.numpy as jnp
from jax import lax
from jax.experimental import pallas as pl
from jax.experimental.pallas import tpu as pltpu
from jax.sharding import PartitionSpec as P

SUB = 8
NEAR = 4
TURNS = (0, 2, 1, 3)
ARRIVE = (0, 3, 1, 2)
STEPS_PER_TURN = 4
VMEM_BYTES = 50 * 1024 * 1024
SMALL_BYTES = 8 * 1024 * 1024


def split_two(full):
    high = full.astype(jnp.bfloat16)
    low = (full - high.astype(jnp.float32)).astype(jnp.bfloat16)
    return high, low


def iota(shape, dim):
    return lax.broadcasted_iota(jnp.int32, shape, dim)


def prepare_kernel(
    root_step, products, pack_ref, mix_out, own_out, vol_out, val_out, drift_out, strike_out
):
    factors = mix_out.shape[0] // SUB
    scen = drift_out.shape[1]
    legs = (pack_ref.shape[0] - factors - 2 * SUB) // 2
    mix = pack_ref[0:factors, 0:factors]
    leg_factor = pack_ref[factors : factors + legs, 0:products]
    leg_weight = pack_ref[factors + legs : factors + 2 * legs, 0:products]
    own = factors + 2 * legs
    own_out[...] = pack_ref[own : own + SUB, :]
    tail = own + SUB
    vol_out[...] = jnp.broadcast_to(pack_ref[tail : tail + 1, :], vol_out.shape)
    base = pack_ref[tail + 1 : tail + 2, 0:factors]
    strike = pack_ref[tail + 2 : tail + 3, 0:products]
    column = lambda row, pick: jnp.sum(jnp.where(pick, row, 0.0), axis=1, keepdims=True)
    same = iota((factors, factors), 0) == iota((factors, factors), 1)
    half_vol = column(base, same) * (0.5 * root_step)
    drift_out[...] = jnp.broadcast_to(0.5 * half_vol * half_vol, (factors, scen))
    square = iota((products, products), 0) == iota((products, products), 1)
    strike_out[...] = jnp.broadcast_to(column(strike, square), (products, scen))

    high, low = split_two(half_vol * mix)
    wide = factors * SUB
    spread = (iota((factors, wide), 0) == iota((factors, wide), 1) // SUB).astype(jnp.bfloat16)
    rows = jnp.concatenate(
        [
            jnp.dot(high, spread, preferred_element_type=jnp.float32),
            jnp.dot(low, spread, preferred_element_type=jnp.float32),
        ],
        axis=1,
    )
    lane = iota((factors, 2 * wide), 1) % SUB
    for path in range(SUB):
        mix_out[path * factors : (path + 1) * factors, :] = jnp.where(
            lane == path, rows, 0.0
        ).astype(jnp.bfloat16)

    ids = iota((factors, products), 0).astype(jnp.float32)
    exposure = jnp.zeros((factors, products), jnp.float32)
    for leg in range(legs):
        hit = leg_factor[leg : leg + 1, :] == ids
        exposure = exposure + jnp.where(hit, leg_weight[leg : leg + 1, :], 0.0)
    high, low = split_two(exposure)
    span = 2 * 3 * factors
    lane = iota((factors, span), 1)
    match = iota((factors, span), 0) == lane % factors
    third = (lane // factors) % 3
    put_high = jnp.logical_and(match, third != 2).astype(jnp.bfloat16)
    put_low = jnp.logical_and(match, third == 2).astype(jnp.bfloat16)
    turned = (((0,), (0,)), ((), ()))
    weights = lax.dot_general(
        high, put_high, turned, preferred_element_type=jnp.float32
    ) + lax.dot_general(low, put_low, turned, preferred_element_type=jnp.float32)
    block = iota((products, span), 1) // (3 * factors)
    for path in range(2):
        val_out[path * products : (path + 1) * products, :] = jnp.where(
            block == path, weights, 0.0
        ).astype(jnp.bfloat16)


def prepare(steps, scen, own, outer_vol, factor_vol, factor_mix, leg_factor, leg_weight, strike):
    factors = factor_mix.shape[0]
    products = strike.shape[0]

    legs = leg_factor.shape[1]
    height = factors + 2 * legs + 2 * SUB
    pack = jnp.zeros((height, scen), jnp.float32)
    start = 0
    for part in (
        factor_mix,
        leg_factor.T.astype(jnp.float32),
        leg_weight.T,
        own,
        outer_vol[None],
        factor_vol[None],
        strike[None],
    ):
        count, width = part.shape
        edges = ((start, height - start - count, 0), (0, scen - width, 0))
        pack = pack + lax.pad(part, jnp.float32(0.0), edges)
        start += count
    shapes = (
        ((SUB * factors, 2 * SUB * factors), jnp.bfloat16),
        ((SUB, scen), jnp.float32),
        ((SUB, scen), jnp.float32),
        ((2 * products, 6 * factors), jnp.bfloat16),
        ((factors, scen), jnp.float32),
        ((products, scen), jnp.float32),
    )
    return pl.pallas_call(
        functools.partial(prepare_kernel, (1.0 / steps) ** 0.5, products),
        out_shape=tuple(pltpu.VMEM(s, d) for s, d in shapes),
        compiler_params=pltpu.CompilerParams(vmem_limit_bytes=SMALL_BYTES),
        cost_estimate=pl.CostEstimate(flops=500_000_000, bytes_accessed=500_000, transcendentals=0),
        name="prepare",
    )(pack)


def relay_kernel(spot_ref, vol_ref, *refs):
    near_refs, out_ref = refs[:-1], refs[-1]
    near = lax.rem(spot_ref[0], NEAR)
    factors = near_refs[1].shape[1]
    vol = vol_ref[0:1, 0:factors]
    out_ref[...] = jnp.zeros_like(out_ref)
    for turn, near_ref in zip(ARRIVE, near_refs):
        begin = pl.multiple_of(jnp.bitwise_xor(near, turn) * SUB, SUB)
        out_ref[pl.ds(begin, SUB), 0:factors] = near_ref[:, 0:factors] * vol


def relay(spot, vol, blocks):
    vmem = pl.BlockSpec(memory_space=pltpu.VMEM)
    return pl.pallas_call(
        relay_kernel,
        out_shape=jax.ShapeDtypeStruct((NEAR * SUB, vol.shape[1]), jnp.float32),
        in_specs=[pl.BlockSpec(memory_space=pltpu.SMEM)] + [vmem] * (1 + len(blocks)),
        out_specs=vmem,
        compiler_params=pltpu.CompilerParams(vmem_limit_bytes=SMALL_BYTES),
        name="relay",
    )(spot, vol, *blocks)


def simulate_kernel(spot_ref, inc_hbm, *refs):
    stacks, refs = refs[: len(TURNS)], refs[len(TURNS) :]
    mix_ref, val_ref, drift_ref, strike_ref = refs[:4]
    out_refs, refs = refs[4 : 4 + len(TURNS)], refs[4 + len(TURNS) :]
    inc, arrived, level, shock, operand, sums, turned = refs
    steps, factors, paths, scen = inc.shape
    products = strike_ref.shape[0]
    unit = 2 * SUB
    units = paths // unit
    pairs = SUB // 2
    near = lax.rem(spot_ref[0], NEAR)
    far = lax.div(spot_ref[0], NEAR)
    wide_turn = STEPS_PER_TURN * products

    def fetch(step):
        return pltpu.make_async_copy(inc_hbm.at[step], inc.at[step], arrived.at[step])

    for step in range(steps):
        fetch(step).start()

    rows = NEAR * SUB
    for turn, stack in zip(ARRIVE, stacks):
        start = pl.multiple_of(jnp.bitwise_xor(far, turn) * rows, rows)
        turned[pl.ds(start, rows), 0:scen] = stack[...]
    begin = jnp.transpose(turned[:, 0:scen])[0:factors, :]
    for path in range(paths):
        level[path] = begin
    operand[...] = jnp.zeros_like(operand)
    sums[0:products, :] = jnp.zeros((products, scen), jnp.float32)

    drift = drift_ref[...]
    strike = strike_ref[...]
    opening = strike * (-1.0 * paths)

    def mix(step, place, slot):
        chunk = inc[step, :, place * unit : (place + 1) * unit, :].astype(jnp.float32)
        sides = [
            chunk[:, side * SUB : (side + 1) * SUB, :].reshape(factors * SUB, scen)
            for side in range(2)
        ]
        normals = jnp.concatenate([x.astype(jnp.bfloat16) for x in sides], axis=1)
        normals = jnp.concatenate([normals, normals], axis=0)
        shock[slot] = jnp.dot(mix_ref[...], normals, preferred_element_type=jnp.float32)

    def grow(place, slot, pair):
        for side in range(2):
            cols = slice(side * scen, (side + 1) * scen)
            for path in range(2):
                row = (2 * pair + path) * factors
                part = shock[slot, row : row + factors, cols]
                spot = place * unit + side * SUB + 2 * pair + path
                old = level[spot]
                wide = jnp.tanh(old) + 2.0
                new = old + wide * (part - drift * wide)
                level[spot] = new
                high, low = split_two(jnp.exp(new))
                base = path * 3 * factors
                operand[slot, pair, base : base + factors, cols] = high
                operand[slot, pair, base + factors : base + 2 * factors, cols] = low
                operand[slot, pair, base + 2 * factors : base + 3 * factors, cols] = high

    def value(slot, pair):
        return jnp.dot(val_ref[...], operand[slot, pair], preferred_element_type=jnp.float32)

    def fold(acc, values):
        for path in range(2):
            for side in range(2):
                piece = values[
                    path * products : (path + 1) * products, side * scen : (side + 1) * scen
                ]
                acc = acc + jnp.maximum(piece, strike)
        return acc

    def send(turn):
        source = pl.multiple_of(turn * wide_turn + products, products)
        turned[...] = jnp.transpose(sums[pl.ds(source, wide_turn), :])
        cols = pl.ds(pl.multiple_of(turn * wide_turn, wide_turn), wide_turn)
        for across, out_ref in zip(TURNS, out_refs):
            other = jnp.bitwise_xor(near, across)
            for place in range(out_ref.shape[0] // SUB):
                start = pl.multiple_of((place * NEAR + other) * SUB, SUB)
                out_ref[place * SUB : (place + 1) * SUB, cols] = turned[pl.ds(start, SUB), :]

    def run(turn, acc):
        for inner in range(STEPS_PER_TURN):
            upcoming = turn * STEPS_PER_TURN + inner + 1

            @pl.when(upcoming < steps)
            def _():
                fetch(upcoming).wait()

        for inner in range(STEPS_PER_TURN):
            step = turn * STEPS_PER_TURN + inner
            for place in range(units):
                slot = place % 2
                if place + 1 < units:
                    mix(step, place + 1, 1 - slot)
                else:
                    mix(jnp.minimum(step + 1, steps - 1), 0, 1 - slot)
                for pair in range(pairs):
                    values = value(1 - slot, pair)
                    grow(place, slot, pair)
                    acc = fold(acc, values)
                if place == 0:
                    sums[pl.ds(pl.multiple_of(step * products, products), products), :] = acc
                    acc = opening
            if inner == 1:
                send(jnp.maximum(turn - 1, 0))
        return acc

    fetch(0).wait()
    mix(0, 0, 0)
    acc = lax.fori_loop(0, steps // STEPS_PER_TURN, run, opening)
    for pair in range(pairs):
        acc = fold(acc, value((units - 1) % 2, pair))
    sums[steps * products :, :] = acc
    send(steps // STEPS_PER_TURN - 1)


def simulate(spot, increments, stacks, weights):
    steps, factors, paths, scen = increments.shape
    products = weights[3].shape[0]
    operands = (*stacks, *weights)
    vmem = pl.BlockSpec(memory_space=pltpu.VMEM)
    shape = (scen // NEAR, steps * products)
    return pl.pallas_call(
        simulate_kernel,
        out_shape=[jax.ShapeDtypeStruct(shape, jnp.float32)] * len(TURNS),
        in_specs=[pl.BlockSpec(memory_space=pltpu.SMEM), pl.BlockSpec(memory_space=pl.ANY)]
        + [vmem] * len(operands),
        out_specs=[vmem] * len(TURNS),
        scratch_shapes=[
            pltpu.VMEM(increments.shape, increments.dtype),
            pltpu.SemaphoreType.DMA((steps,)),
            pltpu.VMEM((paths, factors, scen), jnp.float32),
            pltpu.VMEM((2, SUB * factors, 2 * scen), jnp.float32),
            pltpu.VMEM((2, SUB // 2, 6 * factors, 2 * scen), jnp.bfloat16),
            pltpu.VMEM(((steps + 1) * products, scen), jnp.float32),
            pltpu.VMEM((scen, STEPS_PER_TURN * products), jnp.float32),
        ],
        compiler_params=pltpu.CompilerParams(vmem_limit_bytes=VMEM_BYTES),
        cost_estimate=pl.CostEstimate(
            flops=8_000_000_000, bytes_accessed=8_400_000, transcendentals=0
        ),
        name="simulate",
    )(spot, increments, *operands)


def combine_kernel(spot_ref, *refs):
    parts, outs = refs[: len(TURNS)], refs[len(TURNS) :]
    far = lax.div(spot_ref[0], NEAR)
    for turn, out_ref in zip(TURNS, outs):
        rows = pl.ds(pl.multiple_of(jnp.bitwise_xor(far, turn) * SUB, SUB), SUB)
        total = parts[0][rows, :]
        for part in parts[1:]:
            total = total + part[rows, :]
        out_ref[...] = total


def combine(spot, parts):
    width = parts[0].shape[1]
    vmem = pl.BlockSpec(memory_space=pltpu.VMEM)
    return pl.pallas_call(
        combine_kernel,
        out_shape=[jax.ShapeDtypeStruct((SUB, width), jnp.float32)] * len(TURNS),
        in_specs=[pl.BlockSpec(memory_space=pltpu.SMEM)] + [vmem] * len(TURNS),
        out_specs=[vmem] * len(TURNS),
        compiler_params=pltpu.CompilerParams(vmem_limit_bytes=SMALL_BYTES),
        name="combine",
    )(spot, *parts)


def finish_kernel(paths_total, *refs):
    parts, (reserve_ref, fine_ref, corr_ref) = refs[:-3], refs[-3:]
    products = reserve_ref.shape[1]
    width = parts[0].shape[1]
    half = len(parts) // 2
    mine, theirs = None, None
    for turn, part in zip(TURNS, parts):
        if turn < half:
            mine = part[...] if mine is None else mine + part[...]
        else:
            theirs = part[...] if theirs is None else theirs + part[...]
    reserve = reserve_ref[...]
    limit = jnp.concatenate([reserve] * (width // products), axis=1)
    scale = 1.0 / paths_total
    fine = jnp.maximum((mine + theirs) * scale - limit, 0.0)
    coarse = 0.5 * (
        jnp.maximum(mine * (2.0 * scale) - limit, 0.0)
        + jnp.maximum(theirs * (2.0 * scale) - limit, 0.0)
    )
    gap = fine - coarse

    def over_steps(term):
        lanes = 2 * products
        total = term[:, :lanes]
        for start in range(lanes, width, lanes):
            total = total + term[:, start : start + lanes]
        return (total[:, :products] + total[:, products:]) * (products / width)

    fine_ref[...] = over_steps(fine)
    corr_ref[...] = over_steps(gap)


def per_device(
    increments,
    outer_shock,
    outer_vol,
    factor_vol,
    factor_mix,
    leg_factor,
    leg_weight,
    strike,
    reserve,
):
    step_count, _, paths_here, scen_rows = increments.shape
    path_count = lax.axis_size("path")
    paths_total = paths_here * path_count
    spot = lax.axis_index("path").astype(jnp.int32).reshape(1)

    def swap(value, distance):
        if distance == 0:
            return value
        return lax.ppermute(value, "path", [(i, i ^ distance) for i in range(path_count)])

    own = outer_shock.T
    shared = {turn: swap(own, turn) for turn in ARRIVE}
    mix_w, shared[0], vol, val_w, drift, strike_wide = prepare(
        step_count, scen_rows, own, outer_vol, factor_vol, factor_mix, leg_factor, leg_weight, strike
    )
    rows = relay(spot, vol, [shared[turn] for turn in ARRIVE])
    stacks = [swap(rows, turn * NEAR) for turn in ARRIVE]
    local = simulate(spot, increments, stacks, (mix_w, val_w, drift, strike_wide))
    parts = [swap(value, turn) for value, turn in zip(local, TURNS)]
    sums = combine(spot, parts)
    pieces = [swap(value, turn * NEAR) for value, turn in zip(sums, TURNS)]
    out = jax.ShapeDtypeStruct(reserve.shape, jnp.float32)
    return pl.pallas_call(
        functools.partial(finish_kernel, paths_total),
        out_shape=(out, out),
        compiler_params=pltpu.CompilerParams(vmem_limit_bytes=SMALL_BYTES),
        name="finish",
    )(*pieces, reserve)


def solution(mesh):
    in_specs = (
        P(None, None, "path", "scen"),
        P(None, ("scen", "path")),
        P(),
        P(),
        P(),
        P(),
        P(),
        P(),
        P(("scen", "path"), None),
    )
    out_specs = (P(("scen", "path"), None), P(("scen", "path"), None))
    return jax.shard_map(
        per_device, mesh=mesh, in_specs=in_specs, out_specs=out_specs, check_vma=False
    )
```

```python
import functools
import jax
import jax.numpy as jnp
from jax import lax
from jax.experimental import pallas as pl
from jax.experimental.pallas import tpu as pltpu
from jax.sharding import PartitionSpec as P

SUB = 8
NEAR = 4
TURNS = (0, 2, 1, 3)
ARRIVE = (0, 3, 1, 2)
ARRIVE_FAR = (0, 3, 2, 1)
STEPS_PER_TURN = 4
VMEM_BYTES = 50 * 1024 * 1024
SMALL_BYTES = 8 * 1024 * 1024


def split_two(full):
    high = full.astype(jnp.bfloat16)
    low = (full - high.astype(jnp.float32)).astype(jnp.bfloat16)
    return high, low


def iota(shape, dim):
    return lax.broadcasted_iota(jnp.int32, shape, dim)


def prepare_kernel(
    root_step, products, pack_ref, mix_out, own_out, vol_out, val_out, drift_out, strike_out
):
    factors = mix_out.shape[0] // (2 * SUB)
    scen = drift_out.shape[1]
    legs = (pack_ref.shape[0] - factors - 2 * SUB) // 2
    mix = pack_ref[0:factors, 0:factors]
    leg_factor = pack_ref[factors : factors + legs, 0:products]
    leg_weight = pack_ref[factors + legs : factors + 2 * legs, 0:products]
    own = factors + 2 * legs
    own_out[...] = pack_ref[own : own + SUB, :]
    tail = own + SUB
    vol_out[...] = jnp.broadcast_to(pack_ref[tail : tail + 1, :], vol_out.shape)
    base = pack_ref[tail + 1 : tail + 2, 0:factors]
    strike = pack_ref[tail + 2 : tail + 3, 0:products]
    column = lambda row, pick: jnp.sum(jnp.where(pick, row, 0.0), axis=1, keepdims=True)
    same = iota((factors, factors), 0) == iota((factors, factors), 1)
    half_vol = column(base, same) * (0.5 * root_step)
    drift_out[...] = jnp.broadcast_to(0.5 * half_vol * half_vol, (factors, scen))
    square = iota((products, products), 0) == iota((products, products), 1)
    strike_out[...] = jnp.broadcast_to(column(strike, square), (products, scen))

    high, low = split_two(half_vol * mix)
    wide = factors * SUB
    spread = (iota((factors, wide), 0) == iota((factors, wide), 1) // SUB).astype(jnp.bfloat16)
    rows = jnp.concatenate(
        [
            jnp.dot(high, spread, preferred_element_type=jnp.float32),
            jnp.dot(low, spread, preferred_element_type=jnp.float32),
        ],
        axis=0,
    )
    lane = iota((2 * factors, wide), 1) % SUB
    for path in range(SUB):
        mix_out[path * 2 * factors : (path + 1) * 2 * factors, :] = jnp.where(
            lane == path, rows, 0.0
        ).astype(jnp.bfloat16)

    ids = iota((factors, products), 0).astype(jnp.float32)
    exposure = jnp.zeros((factors, products), jnp.float32)
    for leg in range(legs):
        hit = leg_factor[leg : leg + 1, :] == ids
        exposure = exposure + jnp.where(hit, leg_weight[leg : leg + 1, :], 0.0)
    high, low = split_two(exposure)
    span = 2 * 3 * factors
    lane = iota((factors, span), 1)
    match = iota((factors, span), 0) == lane % factors
    third = (lane // factors) % 3
    put_high = jnp.logical_and(match, third != 2).astype(jnp.bfloat16)
    put_low = jnp.logical_and(match, third == 2).astype(jnp.bfloat16)
    turned = (((0,), (0,)), ((), ()))
    weights = lax.dot_general(
        high, put_high, turned, preferred_element_type=jnp.float32
    ) + lax.dot_general(low, put_low, turned, preferred_element_type=jnp.float32)
    block = iota((products, span), 1) // (3 * factors)
    for path in range(2):
        val_out[path * products : (path + 1) * products, :] = jnp.where(
            block == path, weights, 0.0
        ).astype(jnp.bfloat16)


def prepare(steps, scen, own, outer_vol, factor_vol, factor_mix, leg_factor, leg_weight, strike):
    factors = factor_mix.shape[0]
    products = strike.shape[0]

    legs = leg_factor.shape[1]
    height = factors + 2 * legs + 2 * SUB
    pack = jnp.zeros((height, scen), jnp.float32)
    start = 0
    for part in (
        factor_mix,
        leg_factor.T.astype(jnp.float32),
        leg_weight.T,
        own,
        outer_vol[None],
        factor_vol[None],
        strike[None],
    ):
        count, width = part.shape
        edges = ((start, height - start - count, 0), (0, scen - width, 0))
        pack = pack + lax.pad(part, jnp.float32(0.0), edges)
        start += count
    shapes = (
        ((2 * SUB * factors, SUB * factors), jnp.bfloat16),
        ((SUB, scen), jnp.float32),
        ((SUB, scen), jnp.float32),
        ((2 * products, 6 * factors), jnp.bfloat16),
        ((factors, scen), jnp.float32),
        ((products, scen), jnp.float32),
    )
    return pl.pallas_call(
        functools.partial(prepare_kernel, (1.0 / steps) ** 0.5, products),
        out_shape=tuple(pltpu.VMEM(s, d) for s, d in shapes),
        compiler_params=pltpu.CompilerParams(vmem_limit_bytes=SMALL_BYTES),
        cost_estimate=pl.CostEstimate(flops=500_000_000, bytes_accessed=500_000, transcendentals=0),
        name="prepare",
    )(pack)


def relay_kernel(spot_ref, vol_ref, *refs):
    near_refs, out_ref = refs[:-1], refs[-1]
    near = lax.rem(spot_ref[0], NEAR)
    factors = near_refs[1].shape[1]
    vol = vol_ref[0:1, 0:factors]
    out_ref[...] = jnp.zeros_like(out_ref)
    for turn, near_ref in zip(ARRIVE, near_refs):
        begin = pl.multiple_of(jnp.bitwise_xor(near, turn) * SUB, SUB)
        out_ref[pl.ds(begin, SUB), 0:factors] = near_ref[:, 0:factors] * vol


def relay(spot, vol, blocks):
    vmem = pl.BlockSpec(memory_space=pltpu.VMEM)
    return pl.pallas_call(
        relay_kernel,
        out_shape=jax.ShapeDtypeStruct((NEAR * SUB, vol.shape[1]), jnp.float32),
        in_specs=[pl.BlockSpec(memory_space=pltpu.SMEM)] + [vmem] * (1 + len(blocks)),
        out_specs=vmem,
        compiler_params=pltpu.CompilerParams(vmem_limit_bytes=SMALL_BYTES),
        name="relay",
    )(spot, vol, *blocks)


def simulate_kernel(spot_ref, inc_hbm, *refs):
    stacks, refs = refs[: len(TURNS)], refs[len(TURNS) :]
    mix_ref, val_ref, drift_ref, strike_ref = refs[:4]
    out_refs, refs = refs[4 : 4 + len(TURNS)], refs[4 + len(TURNS) :]
    inc, arrived, level, shock, operand, sums, turned = refs
    steps, factors, paths, scen = inc.shape
    products = strike_ref.shape[0]
    unit = 2 * SUB
    units = paths // unit
    pairs = SUB // 2
    near = lax.rem(spot_ref[0], NEAR)
    far = lax.div(spot_ref[0], NEAR)
    wide_turn = STEPS_PER_TURN * products

    def fetch(step):
        return pltpu.make_async_copy(inc_hbm.at[step], inc.at[step], arrived.at[step])

    for step in range(steps):
        fetch(step).start()

    rows = NEAR * SUB
    for turn, stack in zip(ARRIVE_FAR, stacks):
        start = pl.multiple_of(jnp.bitwise_xor(far, turn) * rows, rows)
        turned[pl.ds(start, rows), 0:scen] = stack[...]
    begin = jnp.transpose(turned[:, 0:scen])[0:factors, :]
    for path in range(paths):
        level[path] = begin
    operand[...] = jnp.zeros_like(operand)
    sums[0:products, :] = jnp.zeros((products, scen), jnp.float32)

    drift = drift_ref[...]
    strike = strike_ref[...]
    opening = strike * (-1.0 * paths)

    def mix(step, place, slot):
        chunk = inc[step, :, place * unit : (place + 1) * unit, :].astype(jnp.float32)
        sides = [
            chunk[:, side * SUB : (side + 1) * SUB, :].reshape(factors * SUB, scen)
            for side in range(2)
        ]
        normals = jnp.concatenate([x.astype(jnp.bfloat16) for x in sides], axis=1)
        both = jnp.dot(mix_ref[...], normals, preferred_element_type=jnp.float32)
        for path in range(SUB):
            row = 2 * path * factors
            shock[slot, path * factors : (path + 1) * factors, :] = (
                both[row : row + factors] + both[row + factors : row + 2 * factors]
            )

    def grow(place, slot, pair):
        for side in range(2):
            cols = slice(side * scen, (side + 1) * scen)
            for path in range(2):
                row = (2 * pair + path) * factors
                part = shock[slot, row : row + factors, cols]
                spot = place * unit + side * SUB + 2 * pair + path
                old = level[spot]
                wide = jnp.tanh(old) + 2.0
                new = old + wide * (part - drift * wide)
                level[spot] = new
                high, low = split_two(jnp.exp(new))
                base = path * 2 * factors
                operand[slot, pair, base : base + factors, cols] = high
                operand[slot, pair, base + factors : base + 2 * factors, cols] = low

    def value(slot, pair):
        pieces = []
        for path in range(2):
            base = path * 2 * factors
            pieces.append(operand[slot, pair, base : base + 2 * factors, :])
            pieces.append(operand[slot, pair, base : base + factors, :])
        stacked = jnp.concatenate(pieces, axis=0)
        return jnp.dot(val_ref[...], stacked, preferred_element_type=jnp.float32)

    def fold(acc, values):
        for path in range(2):
            for side in range(2):
                piece = values[
                    path * products : (path + 1) * products, side * scen : (side + 1) * scen
                ]
                acc = acc + jnp.maximum(piece, strike)
        return acc

    def send(turn):
        source = pl.multiple_of(turn * wide_turn + products, products)
        turned[...] = jnp.transpose(sums[pl.ds(source, wide_turn), :])
        cols = pl.ds(pl.multiple_of(turn * wide_turn, wide_turn), wide_turn)
        for across, out_ref in zip(TURNS, out_refs):
            other = jnp.bitwise_xor(near, across)
            for place in range(out_ref.shape[0] // SUB):
                start = pl.multiple_of((place * NEAR + other) * SUB, SUB)
                out_ref[place * SUB : (place + 1) * SUB, cols] = turned[pl.ds(start, SUB), :]

    def run(turn, acc):
        for inner in range(STEPS_PER_TURN):
            upcoming = turn * STEPS_PER_TURN + inner + 1

            @pl.when(upcoming < steps)
            def _():
                fetch(upcoming).wait()

        for inner in range(STEPS_PER_TURN):
            step = turn * STEPS_PER_TURN + inner
            for place in range(units):
                slot = place % 2
                if place + 1 < units:
                    mix(step, place + 1, 1 - slot)
                else:
                    mix(jnp.minimum(step + 1, steps - 1), 0, 1 - slot)
                for pair in range(pairs):
                    values = value(1 - slot, pair)
                    grow(place, slot, pair)
                    acc = fold(acc, values)
                if place == 0:
                    sums[pl.ds(pl.multiple_of(step * products, products), products), :] = acc
                    acc = opening
            if inner == 1:
                send(jnp.maximum(turn - 1, 0))
        return acc

    fetch(0).wait()
    mix(0, 0, 0)
    acc = lax.fori_loop(0, steps // STEPS_PER_TURN, run, opening)
    for pair in range(pairs):
        acc = fold(acc, value((units - 1) % 2, pair))
    sums[steps * products :, :] = acc
    send(steps // STEPS_PER_TURN - 1)


def simulate(spot, increments, stacks, weights):
    steps, factors, paths, scen = increments.shape
    products = weights[3].shape[0]
    operands = (*stacks, *weights)
    vmem = pl.BlockSpec(memory_space=pltpu.VMEM)
    shape = (scen // NEAR, steps * products)
    return pl.pallas_call(
        simulate_kernel,
        out_shape=[jax.ShapeDtypeStruct(shape, jnp.float32)] * len(TURNS),
        in_specs=[pl.BlockSpec(memory_space=pltpu.SMEM), pl.BlockSpec(memory_space=pl.ANY)]
        + [vmem] * len(operands),
        out_specs=[vmem] * len(TURNS),
        scratch_shapes=[
            pltpu.VMEM(increments.shape, increments.dtype),
            pltpu.SemaphoreType.DMA((steps,)),
            pltpu.VMEM((paths, factors, scen), jnp.float32),
            pltpu.VMEM((2, SUB * factors, 2 * scen), jnp.float32),
            pltpu.VMEM((2, SUB // 2, 4 * factors, 2 * scen), jnp.bfloat16),
            pltpu.VMEM(((steps + 1) * products, scen), jnp.float32),
            pltpu.VMEM((scen, STEPS_PER_TURN * products), jnp.float32),
        ],
        compiler_params=pltpu.CompilerParams(vmem_limit_bytes=VMEM_BYTES),
        cost_estimate=pl.CostEstimate(
            flops=8_000_000_000, bytes_accessed=8_400_000, transcendentals=0
        ),
        name="simulate",
    )(spot, increments, *operands)


def combine_kernel(spot_ref, *refs):
    parts, outs = refs[: len(TURNS)], refs[len(TURNS) :]
    far = lax.div(spot_ref[0], NEAR)
    for turn, out_ref in zip(TURNS, outs):
        rows = pl.ds(pl.multiple_of(jnp.bitwise_xor(far, turn) * SUB, SUB), SUB)
        total = parts[0][rows, :]
        for part in parts[1:]:
            total = total + part[rows, :]
        out_ref[...] = total


def combine(spot, parts):
    width = parts[0].shape[1]
    vmem = pl.BlockSpec(memory_space=pltpu.VMEM)
    return pl.pallas_call(
        combine_kernel,
        out_shape=[jax.ShapeDtypeStruct((SUB, width), jnp.float32)] * len(TURNS),
        in_specs=[pl.BlockSpec(memory_space=pltpu.SMEM)] + [vmem] * len(TURNS),
        out_specs=[vmem] * len(TURNS),
        compiler_params=pltpu.CompilerParams(vmem_limit_bytes=SMALL_BYTES),
        name="combine",
    )(spot, *parts)


def finish_kernel(paths_total, *refs):
    parts, (reserve_ref, fine_ref, corr_ref) = refs[:-3], refs[-3:]
    products = reserve_ref.shape[1]
    width = parts[0].shape[1]
    half = len(parts) // 2
    mine, theirs = None, None
    for turn, part in zip(TURNS, parts):
        if turn < half:
            mine = part[...] if mine is None else mine + part[...]
        else:
            theirs = part[...] if theirs is None else theirs + part[...]
    reserve = reserve_ref[...]
    limit = jnp.concatenate([reserve] * (width // products), axis=1)
    scale = 1.0 / paths_total
    fine = jnp.maximum((mine + theirs) * scale - limit, 0.0)
    coarse = 0.5 * (
        jnp.maximum(mine * (2.0 * scale) - limit, 0.0)
        + jnp.maximum(theirs * (2.0 * scale) - limit, 0.0)
    )
    gap = fine - coarse

    def over_steps(term):
        lanes = 2 * products
        total = term[:, :lanes]
        for start in range(lanes, width, lanes):
            total = total + term[:, start : start + lanes]
        return (total[:, :products] + total[:, products:]) * (products / width)

    fine_ref[...] = over_steps(fine)
    corr_ref[...] = over_steps(gap)


def per_device(
    increments,
    outer_shock,
    outer_vol,
    factor_vol,
    factor_mix,
    leg_factor,
    leg_weight,
    strike,
    reserve,
):
    step_count, _, paths_here, scen_rows = increments.shape
    path_count = lax.axis_size("path")
    paths_total = paths_here * path_count
    spot = lax.axis_index("path").astype(jnp.int32).reshape(1)

    def swap(value, distance):
        if distance == 0:
            return value
        return lax.ppermute(value, "path", [(i, i ^ distance) for i in range(path_count)])

    own = outer_shock.T
    shared = {turn: swap(own, turn) for turn in ARRIVE}
    mix_w, shared[0], vol, val_w, drift, strike_wide = prepare(
        step_count, scen_rows, own, outer_vol, factor_vol, factor_mix, leg_factor, leg_weight, strike
    )
    rows = relay(spot, vol, [shared[turn] for turn in ARRIVE])
    stacks = [swap(rows, turn * NEAR) for turn in ARRIVE_FAR]
    local = simulate(spot, increments, stacks, (mix_w, val_w, drift, strike_wide))
    parts = [swap(value, turn) for value, turn in zip(local, TURNS)]
    sums = combine(spot, parts)
    pieces = [swap(value, turn * NEAR) for value, turn in zip(sums, TURNS)]
    out = jax.ShapeDtypeStruct(reserve.shape, jnp.float32)
    return pl.pallas_call(
        functools.partial(finish_kernel, paths_total),
        out_shape=(out, out),
        compiler_params=pltpu.CompilerParams(vmem_limit_bytes=SMALL_BYTES),
        name="finish",
    )(*pieces, reserve)


def solution(mesh):
    in_specs = (
        P(None, None, "path", "scen"),
        P(None, ("scen", "path")),
        P(),
        P(),
        P(),
        P(),
        P(),
        P(),
        P(("scen", "path"), None),
    )
    out_specs = (P(("scen", "path"), None), P(("scen", "path"), None))
    return jax.shard_map(
        per_device, mesh=mesh, in_specs=in_specs, out_specs=out_specs, check_vma=False
    )
```

```python
import functools
import jax
import jax.numpy as jnp
from jax import lax
from jax.experimental import pallas as pl
from jax.experimental.pallas import tpu as pltpu
from jax.sharding import PartitionSpec as P

SUB = 8
NEAR = 4
TURNS = (0, 2, 1, 3)
ARRIVE = (0, 3, 1, 2)
ARRIVE_FAR = (0, 3, 2, 1)
STEPS_PER_TURN = 4
VMEM_BYTES = 49 * 1024 * 1024
SMALL_BYTES = 8 * 1024 * 1024


def split_two(full):
    high = full.astype(jnp.bfloat16)
    low = (full - high.astype(jnp.float32)).astype(jnp.bfloat16)
    return high, low


def iota(shape, dim):
    return lax.broadcasted_iota(jnp.int32, shape, dim)


def prepare_kernel(
    root_step, products, pack_ref, mix_out, own_out, vol_out, val_out, drift_out, strike_out
):
    factors = mix_out.shape[0] // (2 * SUB)
    scen = drift_out.shape[1]
    legs = (pack_ref.shape[0] - factors - 2 * SUB) // 2
    mix = pack_ref[0:factors, 0:factors]
    leg_factor = pack_ref[factors : factors + legs, 0:products]
    leg_weight = pack_ref[factors + legs : factors + 2 * legs, 0:products]
    own = factors + 2 * legs
    own_out[...] = pack_ref[own : own + SUB, :]
    tail = own + SUB
    vol_out[...] = jnp.broadcast_to(pack_ref[tail : tail + 1, :], vol_out.shape)
    base = pack_ref[tail + 1 : tail + 2, 0:factors]
    strike = pack_ref[tail + 2 : tail + 3, 0:products]
    column = lambda row, pick: jnp.sum(jnp.where(pick, row, 0.0), axis=1, keepdims=True)
    same = iota((factors, factors), 0) == iota((factors, factors), 1)
    half_vol = column(base, same) * (0.5 * root_step)
    drift_out[...] = jnp.broadcast_to(0.5 * half_vol * half_vol, (factors, scen))
    square = iota((products, products), 0) == iota((products, products), 1)
    strike_out[...] = jnp.broadcast_to(column(strike, square), (products, scen))

    high, low = split_two(half_vol * mix)
    wide = factors * SUB
    spread = (iota((factors, wide), 0) == iota((factors, wide), 1) // SUB).astype(jnp.bfloat16)
    rows = jnp.concatenate(
        [
            jnp.dot(high, spread, preferred_element_type=jnp.float32),
            jnp.dot(low, spread, preferred_element_type=jnp.float32),
        ],
        axis=0,
    )
    lane = iota((2 * factors, wide), 1) % SUB
    for path in range(SUB):
        mix_out[path * 2 * factors : (path + 1) * 2 * factors, :] = jnp.where(
            lane == path, rows, 0.0
        ).astype(jnp.bfloat16)

    ids = iota((factors, products), 0).astype(jnp.float32)
    exposure = jnp.zeros((factors, products), jnp.float32)
    for leg in range(legs):
        hit = leg_factor[leg : leg + 1, :] == ids
        exposure = exposure + jnp.where(hit, leg_weight[leg : leg + 1, :], 0.0)
    high, low = split_two(exposure)
    span = 2 * 3 * factors
    lane = iota((factors, span), 1)
    match = iota((factors, span), 0) == lane % factors
    third = (lane // factors) % 3
    put_high = jnp.logical_and(match, third != 2).astype(jnp.bfloat16)
    put_low = jnp.logical_and(match, third == 2).astype(jnp.bfloat16)
    turned = (((0,), (0,)), ((), ()))
    weights = lax.dot_general(
        high, put_high, turned, preferred_element_type=jnp.float32
    ) + lax.dot_general(low, put_low, turned, preferred_element_type=jnp.float32)
    block = iota((products, span), 1) // (3 * factors)
    for path in range(2):
        val_out[path * products : (path + 1) * products, :] = jnp.where(
            block == path, weights, 0.0
        ).astype(jnp.bfloat16)


def prepare(steps, scen, own, outer_vol, factor_vol, factor_mix, leg_factor, leg_weight, strike):
    factors = factor_mix.shape[0]
    products = strike.shape[0]

    legs = leg_factor.shape[1]
    height = factors + 2 * legs + 2 * SUB
    pack = jnp.zeros((height, scen), jnp.float32)
    start = 0
    for part in (
        factor_mix,
        leg_factor.T.astype(jnp.float32),
        leg_weight.T,
        own,
        outer_vol[None],
        factor_vol[None],
        strike[None],
    ):
        count, width = part.shape
        edges = ((start, height - start - count, 0), (0, scen - width, 0))
        pack = pack + lax.pad(part, jnp.float32(0.0), edges)
        start += count
    shapes = (
        ((2 * SUB * factors, SUB * factors), jnp.bfloat16),
        ((SUB, scen), jnp.float32),
        ((SUB, scen), jnp.float32),
        ((2 * products, 6 * factors), jnp.bfloat16),
        ((factors, scen), jnp.float32),
        ((products, scen), jnp.float32),
    )
    return pl.pallas_call(
        functools.partial(prepare_kernel, (1.0 / steps) ** 0.5, products),
        out_shape=tuple(pltpu.VMEM(s, d) for s, d in shapes),
        compiler_params=pltpu.CompilerParams(vmem_limit_bytes=SMALL_BYTES),
        cost_estimate=pl.CostEstimate(flops=500_000_000, bytes_accessed=500_000, transcendentals=0),
        name="prepare",
    )(pack)


def relay_kernel(spot_ref, vol_ref, *refs):
    near_refs, out_ref = refs[:-1], refs[-1]
    near = lax.rem(spot_ref[0], NEAR)
    factors = near_refs[1].shape[1]
    vol = vol_ref[0:1, 0:factors]
    out_ref[...] = jnp.zeros_like(out_ref)
    for turn, near_ref in zip(ARRIVE, near_refs):
        begin = pl.multiple_of(jnp.bitwise_xor(near, turn) * SUB, SUB)
        out_ref[pl.ds(begin, SUB), 0:factors] = near_ref[:, 0:factors] * vol


def relay(spot, vol, blocks):
    vmem = pl.BlockSpec(memory_space=pltpu.VMEM)
    return pl.pallas_call(
        relay_kernel,
        out_shape=jax.ShapeDtypeStruct((NEAR * SUB, vol.shape[1]), jnp.float32),
        in_specs=[pl.BlockSpec(memory_space=pltpu.SMEM)] + [vmem] * (1 + len(blocks)),
        out_specs=vmem,
        compiler_params=pltpu.CompilerParams(vmem_limit_bytes=SMALL_BYTES),
        name="relay",
    )(spot, vol, *blocks)


def mix_unit(inc, mix_ref, step, place, target, slot):
    _, factors, _, scen = inc.shape
    unit = 2 * SUB
    chunk = inc[step, :, place * unit : (place + 1) * unit, :].astype(jnp.float32)
    sides = [
        chunk[:, side * SUB : (side + 1) * SUB, :].reshape(factors * SUB, scen) for side in range(2)
    ]
    normals = jnp.concatenate([x.astype(jnp.bfloat16) for x in sides], axis=1)
    both = jnp.dot(mix_ref[...], normals, preferred_element_type=jnp.float32)
    for path in range(SUB):
        row = 2 * path * factors
        target[slot, path * factors : (path + 1) * factors, :] = (
            both[row : row + factors] + both[row + factors : row + 2 * factors]
        )


def ahead_kernel(inc_hbm, mix_ref, after_ref, shock_out, inc, arrived):
    steps, _, paths, _ = inc.shape
    units = paths // (2 * SUB)

    def fetch(step):
        return pltpu.make_async_copy(inc_hbm.at[step], inc.at[step], arrived.at[step])

    for step in range(steps):
        fetch(step).start()
    for step in range(steps):
        fetch(step).wait()
        for place in range(units):
            mix_unit(inc, mix_ref, step, place, shock_out, step * units + place)


def ahead(increments, mix_w, after):
    _, factors, paths, scen = increments.shape
    steps = STEPS_PER_TURN
    units = paths // (2 * SUB)
    vmem = pl.BlockSpec(memory_space=pltpu.VMEM)
    return pl.pallas_call(
        ahead_kernel,
        out_shape=pltpu.VMEM((steps * units, SUB * factors, 2 * scen), jnp.float32),
        in_specs=[pl.BlockSpec(memory_space=pl.ANY), vmem, vmem],
        out_specs=vmem,
        scratch_shapes=[
            pltpu.VMEM((steps, factors, paths, scen), increments.dtype),
            pltpu.SemaphoreType.DMA((steps,)),
        ],
        compiler_params=pltpu.CompilerParams(vmem_limit_bytes=VMEM_BYTES),
        cost_estimate=pl.CostEstimate(
            flops=2_000_000_000, bytes_accessed=2_100_000, transcendentals=0
        ),
        name="ahead",
    )(increments, mix_w, after)


def simulate_kernel(spot_ref, inc_hbm, *refs):
    stacks, refs = refs[: len(TURNS)], refs[len(TURNS) :]
    early, mix_ref, val_ref, drift_ref, strike_ref = refs[:5]
    out_refs, refs = refs[5 : 5 + len(TURNS)], refs[5 + len(TURNS) :]
    inc, arrived, level, shock, operand, sums, turned = refs
    steps, factors, paths, scen = inc.shape
    products = strike_ref.shape[0]
    unit = 2 * SUB
    units = paths // unit
    pairs = SUB // 2
    near = lax.rem(spot_ref[0], NEAR)
    far = lax.div(spot_ref[0], NEAR)
    wide_turn = STEPS_PER_TURN * products

    def fetch(step):
        return pltpu.make_async_copy(inc_hbm.at[step], inc.at[step], arrived.at[step])

    for step in range(STEPS_PER_TURN, steps):
        fetch(step).start()

    rows = NEAR * SUB
    for turn, stack in zip(ARRIVE_FAR, stacks):
        start = pl.multiple_of(jnp.bitwise_xor(far, turn) * rows, rows)
        turned[pl.ds(start, rows), 0:scen] = stack[...]
    begin = jnp.transpose(turned[:, 0:scen])[0:factors, :]
    for path in range(paths):
        level[path] = begin
    operand[...] = jnp.zeros_like(operand)
    sums[0:products, :] = jnp.zeros((products, scen), jnp.float32)

    drift = drift_ref[...]
    strike = strike_ref[...]
    opening = strike * (-1.0 * paths)

    def grow(source, index, place, slot, pair):
        for side in range(2):
            cols = slice(side * scen, (side + 1) * scen)
            for path in range(2):
                row = (2 * pair + path) * factors
                part = source[index, row : row + factors, cols]
                spot = place * unit + side * SUB + 2 * pair + path
                old = level[spot]
                wide = jnp.tanh(old) + 2.0
                new = old + wide * (part - drift * wide)
                level[spot] = new
                high, low = split_two(jnp.exp(new))
                base = path * 2 * factors
                operand[slot, pair, base : base + factors, cols] = high
                operand[slot, pair, base + factors : base + 2 * factors, cols] = low

    def value(slot, pair):
        pieces = []
        for path in range(2):
            base = path * 2 * factors
            pieces.append(operand[slot, pair, base : base + 2 * factors, :])
            pieces.append(operand[slot, pair, base : base + factors, :])
        stacked = jnp.concatenate(pieces, axis=0)
        return jnp.dot(val_ref[...], stacked, preferred_element_type=jnp.float32)

    def fold(acc, values):
        for path in range(2):
            for side in range(2):
                piece = values[
                    path * products : (path + 1) * products, side * scen : (side + 1) * scen
                ]
                acc = acc + jnp.maximum(piece, strike)
        return acc

    def send(turn):
        source = pl.multiple_of(turn * wide_turn + products, products)
        turned[...] = jnp.transpose(sums[pl.ds(source, wide_turn), :])
        cols = pl.ds(pl.multiple_of(turn * wide_turn, wide_turn), wide_turn)
        for across, out_ref in zip(TURNS, out_refs):
            other = jnp.bitwise_xor(near, across)
            for place in range(out_ref.shape[0] // SUB):
                start = pl.multiple_of((place * NEAR + other) * SUB, SUB)
                out_ref[place * SUB : (place + 1) * SUB, cols] = turned[pl.ds(start, SUB), :]

    def run(turn, acc, ready):
        if not ready:
            for inner in range(STEPS_PER_TURN):
                upcoming = turn * STEPS_PER_TURN + inner + 1

                @pl.when(upcoming < steps)
                def _():
                    fetch(upcoming).wait()

        for inner in range(STEPS_PER_TURN):
            step = turn * STEPS_PER_TURN + inner
            for place in range(units):
                slot = place % 2
                if place + 1 < units:
                    if not ready:
                        mix_unit(inc, mix_ref, step, place + 1, shock, 1 - slot)
                elif not ready:
                    mix_unit(inc, mix_ref, jnp.minimum(step + 1, steps - 1), 0, shock, 1 - slot)
                elif inner + 1 == STEPS_PER_TURN:
                    fetch(STEPS_PER_TURN).wait()
                    mix_unit(inc, mix_ref, STEPS_PER_TURN, 0, shock, 1 - slot)
                for pair in range(pairs):
                    values = value(1 - slot, pair)
                    if ready:
                        grow(early, inner * units + place, place, slot, pair)
                    else:
                        grow(shock, slot, place, slot, pair)
                    acc = fold(acc, values)
                if place == 0:
                    where = step * products
                    if not ready:
                        where = pl.multiple_of(where, products)
                    sums[pl.ds(where, products), :] = acc
                    acc = opening
            if inner == 1 and not ready:
                send(turn - 1)
        return acc

    acc = run(0, opening, True)
    acc = lax.fori_loop(
        1, steps // STEPS_PER_TURN, lambda turn, acc: run(turn, acc, False), acc
    )
    for pair in range(pairs):
        acc = fold(acc, value((units - 1) % 2, pair))
    sums[steps * products :, :] = acc
    send(steps // STEPS_PER_TURN - 1)


def simulate(spot, increments, stacks, early, weights):
    steps, factors, paths, scen = increments.shape
    products = weights[3].shape[0]
    operands = (*stacks, early, *weights)
    vmem = pl.BlockSpec(memory_space=pltpu.VMEM)
    shape = (scen // NEAR, steps * products)
    return pl.pallas_call(
        simulate_kernel,
        out_shape=[jax.ShapeDtypeStruct(shape, jnp.float32)] * len(TURNS),
        in_specs=[pl.BlockSpec(memory_space=pltpu.SMEM), pl.BlockSpec(memory_space=pl.ANY)]
        + [vmem] * len(operands),
        out_specs=[vmem] * len(TURNS),
        scratch_shapes=[
            pltpu.VMEM(increments.shape, increments.dtype),
            pltpu.SemaphoreType.DMA((steps,)),
            pltpu.VMEM((paths, factors, scen), jnp.float32),
            pltpu.VMEM((2, SUB * factors, 2 * scen), jnp.float32),
            pltpu.VMEM((2, SUB // 2, 4 * factors, 2 * scen), jnp.bfloat16),
            pltpu.VMEM(((steps + 1) * products, scen), jnp.float32),
            pltpu.VMEM((scen, STEPS_PER_TURN * products), jnp.float32),
        ],
        compiler_params=pltpu.CompilerParams(vmem_limit_bytes=VMEM_BYTES),
        cost_estimate=pl.CostEstimate(
            flops=8_000_000_000, bytes_accessed=8_400_000, transcendentals=0
        ),
        name="simulate",
    )(spot, increments, *operands)


def combine_kernel(spot_ref, *refs):
    parts, outs = refs[: len(TURNS)], refs[len(TURNS) :]
    far = lax.div(spot_ref[0], NEAR)
    for turn, out_ref in zip(TURNS, outs):
        rows = pl.ds(pl.multiple_of(jnp.bitwise_xor(far, turn) * SUB, SUB), SUB)
        total = parts[0][rows, :]
        for part in parts[1:]:
            total = total + part[rows, :]
        out_ref[...] = total


def combine(spot, parts):
    width = parts[0].shape[1]
    vmem = pl.BlockSpec(memory_space=pltpu.VMEM)
    return pl.pallas_call(
        combine_kernel,
        out_shape=[jax.ShapeDtypeStruct((SUB, width), jnp.float32)] * len(TURNS),
        in_specs=[pl.BlockSpec(memory_space=pltpu.SMEM)] + [vmem] * len(TURNS),
        out_specs=[vmem] * len(TURNS),
        compiler_params=pltpu.CompilerParams(vmem_limit_bytes=SMALL_BYTES),
        name="combine",
    )(spot, *parts)


def finish_kernel(paths_total, *refs):
    parts, (reserve_ref, fine_ref, corr_ref) = refs[:-3], refs[-3:]
    products = reserve_ref.shape[1]
    width = parts[0].shape[1]
    half = len(parts) // 2
    mine, theirs = None, None
    for turn, part in zip(TURNS, parts):
        if turn < half:
            mine = part[...] if mine is None else mine + part[...]
        else:
            theirs = part[...] if theirs is None else theirs + part[...]
    reserve = reserve_ref[...]
    limit = jnp.concatenate([reserve] * (width // products), axis=1)
    scale = 1.0 / paths_total
    fine = jnp.maximum((mine + theirs) * scale - limit, 0.0)
    coarse = 0.5 * (
        jnp.maximum(mine * (2.0 * scale) - limit, 0.0)
        + jnp.maximum(theirs * (2.0 * scale) - limit, 0.0)
    )
    gap = fine - coarse

    def over_steps(term):
        lanes = 2 * products
        total = term[:, :lanes]
        for start in range(lanes, width, lanes):
            total = total + term[:, start : start + lanes]
        return (total[:, :products] + total[:, products:]) * (products / width)

    fine_ref[...] = over_steps(fine)
    corr_ref[...] = over_steps(gap)


def per_device(
    increments,
    outer_shock,
    outer_vol,
    factor_vol,
    factor_mix,
    leg_factor,
    leg_weight,
    strike,
    reserve,
):
    step_count, _, paths_here, scen_rows = increments.shape
    path_count = lax.axis_size("path")
    paths_total = paths_here * path_count
    spot = lax.axis_index("path").astype(jnp.int32).reshape(1)

    def swap(value, distance):
        if distance == 0:
            return value
        return lax.ppermute(value, "path", [(i, i ^ distance) for i in range(path_count)])

    own = outer_shock.T
    shared = {turn: swap(own, turn) for turn in ARRIVE}
    mix_w, shared[0], vol, val_w, drift, strike_wide = prepare(
        step_count, scen_rows, own, outer_vol, factor_vol, factor_mix, leg_factor, leg_weight, strike
    )
    rows = relay(spot, vol, [shared[turn] for turn in ARRIVE])
    stacks = [swap(rows, turn * NEAR) for turn in ARRIVE_FAR]
    early = ahead(increments, mix_w, rows)
    local = simulate(spot, increments, stacks, early, (mix_w, val_w, drift, strike_wide))
    parts = [swap(value, turn) for value, turn in zip(local, TURNS)]
    sums = combine(spot, parts)
    pieces = [swap(value, turn * NEAR) for value, turn in zip(sums, TURNS)]
    out = jax.ShapeDtypeStruct(reserve.shape, jnp.float32)
    return pl.pallas_call(
        functools.partial(finish_kernel, paths_total),
        out_shape=(out, out),
        compiler_params=pltpu.CompilerParams(vmem_limit_bytes=SMALL_BYTES),
        name="finish",
    )(*pieces, reserve)


def solution(mesh):
    in_specs = (
        P(None, None, "path", "scen"),
        P(None, ("scen", "path")),
        P(),
        P(),
        P(),
        P(),
        P(),
        P(),
        P(("scen", "path"), None),
    )
    out_specs = (P(("scen", "path"), None), P(("scen", "path"), None))
    return jax.shard_map(
        per_device, mesh=mesh, in_specs=in_specs, out_specs=out_specs, check_vma=False
    )
```

```python
import functools
import jax
import jax.numpy as jnp
from jax import lax
from jax.experimental import pallas as pl
from jax.experimental.pallas import tpu as pltpu
from jax.sharding import PartitionSpec as P

SUB = 8
NEAR = 4
TURNS = (0, 2, 1, 3)
FAR_TURNS = (0, 1, 2, 3)
ARRIVE = (0, 3, 1, 2)
ARRIVE_FAR = (0, 3, 2, 1)
STEPS_PER_TURN = 4
VMEM_BYTES = 49 * 1024 * 1024
SMALL_BYTES = 8 * 1024 * 1024


def split_two(full):
    high = full.astype(jnp.bfloat16)
    low = (full - high.astype(jnp.float32)).astype(jnp.bfloat16)
    return high, low


def iota(shape, dim):
    return lax.broadcasted_iota(jnp.int32, shape, dim)


def prepare_kernel(
    root_step, products, pack_ref, mix_out, own_out, vol_out, val_out, drift_out, strike_out
):
    factors = mix_out.shape[0] // (2 * SUB)
    scen = drift_out.shape[1]
    legs = (pack_ref.shape[0] - factors - 2 * SUB) // 2
    mix = pack_ref[0:factors, 0:factors]
    leg_factor = pack_ref[factors : factors + legs, 0:products]
    leg_weight = pack_ref[factors + legs : factors + 2 * legs, 0:products]
    own = factors + 2 * legs
    own_out[...] = pack_ref[own : own + SUB, :]
    tail = own + SUB
    vol_out[...] = jnp.broadcast_to(pack_ref[tail : tail + 1, :], vol_out.shape)
    base = pack_ref[tail + 1 : tail + 2, 0:factors]
    strike = pack_ref[tail + 2 : tail + 3, 0:products]
    column = lambda row, pick: jnp.sum(jnp.where(pick, row, 0.0), axis=1, keepdims=True)
    same = iota((factors, factors), 0) == iota((factors, factors), 1)
    half_vol = column(base, same) * (0.5 * root_step)
    drift_out[...] = jnp.broadcast_to(0.5 * half_vol * half_vol, (factors, scen))
    square = iota((products, products), 0) == iota((products, products), 1)
    strike_out[...] = jnp.broadcast_to(column(strike, square), (products, scen))

    high, low = split_two(half_vol * mix)
    wide = factors * SUB
    spread = (iota((factors, wide), 0) == iota((factors, wide), 1) // SUB).astype(jnp.bfloat16)
    rows = jnp.concatenate(
        [
            jnp.dot(high, spread, preferred_element_type=jnp.float32),
            jnp.dot(low, spread, preferred_element_type=jnp.float32),
        ],
        axis=0,
    )
    lane = iota((2 * factors, wide), 1) % SUB
    for path in range(SUB):
        mix_out[path * 2 * factors : (path + 1) * 2 * factors, :] = jnp.where(
            lane == path, rows, 0.0
        ).astype(jnp.bfloat16)

    ids = iota((factors, products), 0).astype(jnp.float32)
    exposure = jnp.zeros((factors, products), jnp.float32)
    for leg in range(legs):
        hit = leg_factor[leg : leg + 1, :] == ids
        exposure = exposure + jnp.where(hit, leg_weight[leg : leg + 1, :], 0.0)
    high, low = split_two(exposure)
    span = 2 * 3 * factors
    lane = iota((factors, span), 1)
    match = iota((factors, span), 0) == lane % factors
    third = (lane // factors) % 3
    put_high = jnp.logical_and(match, third != 2).astype(jnp.bfloat16)
    put_low = jnp.logical_and(match, third == 2).astype(jnp.bfloat16)
    turned = (((0,), (0,)), ((), ()))
    weights = lax.dot_general(
        high, put_high, turned, preferred_element_type=jnp.float32
    ) + lax.dot_general(low, put_low, turned, preferred_element_type=jnp.float32)
    block = iota((products, span), 1) // (3 * factors)
    for path in range(2):
        val_out[path * products : (path + 1) * products, :] = jnp.where(
            block == path, weights, 0.0
        ).astype(jnp.bfloat16)


def prepare(steps, scen, own, outer_vol, factor_vol, factor_mix, leg_factor, leg_weight, strike):
    factors = factor_mix.shape[0]
    products = strike.shape[0]

    legs = leg_factor.shape[1]
    height = factors + 2 * legs + 2 * SUB
    pack = jnp.zeros((height, scen), jnp.float32)
    start = 0
    for part in (
        factor_mix,
        leg_factor.T.astype(jnp.float32),
        leg_weight.T,
        own,
        outer_vol[None],
        factor_vol[None],
        strike[None],
    ):
        count, width = part.shape
        edges = ((start, height - start - count, 0), (0, scen - width, 0))
        pack = pack + lax.pad(part, jnp.float32(0.0), edges)
        start += count
    shapes = (
        ((2 * SUB * factors, SUB * factors), jnp.bfloat16),
        ((SUB, scen), jnp.float32),
        ((SUB, scen), jnp.float32),
        ((2 * products, 6 * factors), jnp.bfloat16),
        ((factors, scen), jnp.float32),
        ((products, scen), jnp.float32),
    )
    return pl.pallas_call(
        functools.partial(prepare_kernel, (1.0 / steps) ** 0.5, products),
        out_shape=tuple(pltpu.VMEM(s, d) for s, d in shapes),
        compiler_params=pltpu.CompilerParams(vmem_limit_bytes=SMALL_BYTES),
        cost_estimate=pl.CostEstimate(flops=500_000_000, bytes_accessed=500_000, transcendentals=0),
        name="prepare",
    )(pack)


def relay_kernel(spot_ref, vol_ref, *refs):
    near_refs, out_ref = refs[:-1], refs[-1]
    near = lax.rem(spot_ref[0], NEAR)
    factors = near_refs[1].shape[1]
    vol = vol_ref[0:1, 0:factors]
    out_ref[...] = jnp.zeros_like(out_ref)
    for turn, near_ref in zip(ARRIVE, near_refs):
        begin = pl.multiple_of(jnp.bitwise_xor(near, turn) * SUB, SUB)
        out_ref[pl.ds(begin, SUB), 0:factors] = near_ref[:, 0:factors] * vol


def relay(spot, vol, blocks):
    vmem = pl.BlockSpec(memory_space=pltpu.VMEM)
    return pl.pallas_call(
        relay_kernel,
        out_shape=jax.ShapeDtypeStruct((NEAR * SUB, vol.shape[1]), jnp.float32),
        in_specs=[pl.BlockSpec(memory_space=pltpu.SMEM)] + [vmem] * (1 + len(blocks)),
        out_specs=vmem,
        compiler_params=pltpu.CompilerParams(vmem_limit_bytes=SMALL_BYTES),
        name="relay",
    )(spot, vol, *blocks)


def mix_unit(inc, mix_ref, step, place, target, slot):
    _, factors, _, scen = inc.shape
    unit = 2 * SUB
    chunk = inc[step, :, place * unit : (place + 1) * unit, :].astype(jnp.float32)
    sides = [
        chunk[:, side * SUB : (side + 1) * SUB, :].reshape(factors * SUB, scen) for side in range(2)
    ]
    normals = jnp.concatenate([x.astype(jnp.bfloat16) for x in sides], axis=1)
    both = jnp.dot(mix_ref[...], normals, preferred_element_type=jnp.float32)
    for path in range(SUB):
        row = 2 * path * factors
        target[slot, path * factors : (path + 1) * factors, :] = (
            both[row : row + factors] + both[row + factors : row + 2 * factors]
        )


def ahead_kernel(inc_hbm, mix_ref, after_ref, shock_out, inc, arrived):
    steps, _, paths, _ = inc.shape
    units = paths // (2 * SUB)

    def fetch(step):
        return pltpu.make_async_copy(inc_hbm.at[step], inc.at[step], arrived.at[step])

    for step in range(steps):
        fetch(step).start()
    for step in range(steps):
        fetch(step).wait()
        for place in range(units):
            mix_unit(inc, mix_ref, step, place, shock_out, step * units + place)


def ahead(increments, mix_w, after):
    _, factors, paths, scen = increments.shape
    steps = STEPS_PER_TURN
    units = paths // (2 * SUB)
    vmem = pl.BlockSpec(memory_space=pltpu.VMEM)
    return pl.pallas_call(
        ahead_kernel,
        out_shape=pltpu.VMEM((steps * units, SUB * factors, 2 * scen), jnp.float32),
        in_specs=[pl.BlockSpec(memory_space=pl.ANY), vmem, vmem],
        out_specs=vmem,
        scratch_shapes=[
            pltpu.VMEM((steps, factors, paths, scen), increments.dtype),
            pltpu.SemaphoreType.DMA((steps,)),
        ],
        compiler_params=pltpu.CompilerParams(vmem_limit_bytes=VMEM_BYTES),
        cost_estimate=pl.CostEstimate(
            flops=2_000_000_000, bytes_accessed=2_100_000, transcendentals=0
        ),
        name="ahead",
    )(increments, mix_w, after)


def simulate_kernel(spot_ref, inc_hbm, *refs):
    stacks, refs = refs[: len(TURNS)], refs[len(TURNS) :]
    early, mix_ref, val_ref, drift_ref, strike_ref = refs[:5]
    out_refs, refs = refs[5 : 5 + len(TURNS)], refs[5 + len(TURNS) :]
    inc, arrived, level, shock, operand, sums, turned = refs
    steps, factors, paths, scen = inc.shape
    products = strike_ref.shape[0]
    unit = 2 * SUB
    units = paths // unit
    pairs = SUB // 2
    near = lax.rem(spot_ref[0], NEAR)
    far = lax.div(spot_ref[0], NEAR)
    wide_turn = STEPS_PER_TURN * products

    def fetch(step):
        return pltpu.make_async_copy(inc_hbm.at[step], inc.at[step], arrived.at[step])

    for step in range(STEPS_PER_TURN, steps):
        fetch(step).start()

    rows = NEAR * SUB
    for turn, stack in zip(ARRIVE_FAR, stacks):
        start = pl.multiple_of(jnp.bitwise_xor(far, turn) * rows, rows)
        turned[pl.ds(start, rows), 0:scen] = stack[...]
    begin = jnp.transpose(turned[:, 0:scen])[0:factors, :]
    for path in range(paths):
        level[path] = begin
    operand[...] = jnp.zeros_like(operand)
    sums[0:products, :] = jnp.zeros((products, scen), jnp.float32)

    drift = drift_ref[...]
    strike = strike_ref[...]
    opening = strike * (-1.0 * paths)

    def grow(source, index, place, slot, pair):
        for side in range(2):
            cols = slice(side * scen, (side + 1) * scen)
            for path in range(2):
                row = (2 * pair + path) * factors
                part = source[index, row : row + factors, cols]
                spot = place * unit + side * SUB + 2 * pair + path
                old = level[spot]
                wide = jnp.tanh(old) + 2.0
                new = old + wide * (part - drift * wide)
                level[spot] = new
                high, low = split_two(jnp.exp(new))
                base = path * 2 * factors
                operand[slot, pair, base : base + factors, cols] = high
                operand[slot, pair, base + factors : base + 2 * factors, cols] = low

    def value(slot, pair):
        pieces = []
        for path in range(2):
            base = path * 2 * factors
            pieces.append(operand[slot, pair, base : base + 2 * factors, :])
            pieces.append(operand[slot, pair, base : base + factors, :])
        stacked = jnp.concatenate(pieces, axis=0)
        return jnp.dot(val_ref[...], stacked, preferred_element_type=jnp.float32)

    def fold(acc, values):
        for path in range(2):
            for side in range(2):
                piece = values[
                    path * products : (path + 1) * products, side * scen : (side + 1) * scen
                ]
                acc = acc + jnp.maximum(piece, strike)
        return acc

    def send(turn):
        source = pl.multiple_of(turn * wide_turn + products, products)
        turned[...] = jnp.transpose(sums[pl.ds(source, wide_turn), :])
        cols = pl.ds(pl.multiple_of(turn * wide_turn, wide_turn), wide_turn)
        for across, out_ref in zip(TURNS, out_refs):
            other = jnp.bitwise_xor(near, across)
            for place in range(out_ref.shape[0] // SUB):
                start = pl.multiple_of((place * NEAR + other) * SUB, SUB)
                out_ref[place * SUB : (place + 1) * SUB, cols] = turned[pl.ds(start, SUB), :]

    def run(turn, acc, ready):
        if not ready:
            for inner in range(STEPS_PER_TURN):
                upcoming = turn * STEPS_PER_TURN + inner + 1

                @pl.when(upcoming < steps)
                def _():
                    fetch(upcoming).wait()

        for inner in range(STEPS_PER_TURN):
            step = turn * STEPS_PER_TURN + inner
            for place in range(units):
                slot = place % 2
                if place + 1 < units:
                    if not ready:
                        mix_unit(inc, mix_ref, step, place + 1, shock, 1 - slot)
                elif not ready:
                    mix_unit(inc, mix_ref, jnp.minimum(step + 1, steps - 1), 0, shock, 1 - slot)
                elif inner + 1 == STEPS_PER_TURN:
                    fetch(STEPS_PER_TURN).wait()
                    mix_unit(inc, mix_ref, STEPS_PER_TURN, 0, shock, 1 - slot)
                for pair in range(pairs):
                    values = value(1 - slot, pair)
                    if ready:
                        grow(early, inner * units + place, place, slot, pair)
                    else:
                        grow(shock, slot, place, slot, pair)
                    acc = fold(acc, values)
                if place == 0:
                    where = step * products
                    if not ready:
                        where = pl.multiple_of(where, products)
                    sums[pl.ds(where, products), :] = acc
                    acc = opening
            if inner == 1 and not ready:
                send(turn - 1)
        return acc

    acc = run(0, opening, True)
    acc = lax.fori_loop(
        1, steps // STEPS_PER_TURN, lambda turn, acc: run(turn, acc, False), acc
    )
    for pair in range(pairs):
        acc = fold(acc, value((units - 1) % 2, pair))
    sums[steps * products :, :] = acc
    send(steps // STEPS_PER_TURN - 1)


def simulate(spot, increments, stacks, early, weights):
    steps, factors, paths, scen = increments.shape
    products = weights[3].shape[0]
    operands = (*stacks, early, *weights)
    vmem = pl.BlockSpec(memory_space=pltpu.VMEM)
    shape = (scen // NEAR, steps * products)
    return pl.pallas_call(
        simulate_kernel,
        out_shape=[jax.ShapeDtypeStruct(shape, jnp.float32)] * len(TURNS),
        in_specs=[pl.BlockSpec(memory_space=pltpu.SMEM), pl.BlockSpec(memory_space=pl.ANY)]
        + [vmem] * len(operands),
        out_specs=[vmem] * len(TURNS),
        scratch_shapes=[
            pltpu.VMEM(increments.shape, increments.dtype),
            pltpu.SemaphoreType.DMA((steps,)),
            pltpu.VMEM((paths, factors, scen), jnp.float32),
            pltpu.VMEM((2, SUB * factors, 2 * scen), jnp.float32),
            pltpu.VMEM((2, SUB // 2, 4 * factors, 2 * scen), jnp.bfloat16),
            pltpu.VMEM(((steps + 1) * products, scen), jnp.float32),
            pltpu.VMEM((scen, STEPS_PER_TURN * products), jnp.float32),
        ],
        compiler_params=pltpu.CompilerParams(vmem_limit_bytes=VMEM_BYTES),
        cost_estimate=pl.CostEstimate(
            flops=8_000_000_000, bytes_accessed=8_400_000, transcendentals=0
        ),
        name="simulate",
    )(spot, increments, *operands)


def combine_kernel(spot_ref, *refs):
    parts, outs = refs[: len(TURNS)], refs[len(TURNS) :]
    far = lax.div(spot_ref[0], NEAR)
    for turn, out_ref in zip(FAR_TURNS, outs):
        rows = pl.ds(pl.multiple_of(jnp.bitwise_xor(far, turn) * SUB, SUB), SUB)
        total = parts[0][rows, :]
        for part in parts[1:]:
            total = total + part[rows, :]
        out_ref[...] = total


def combine(spot, parts):
    width = parts[0].shape[1]
    vmem = pl.BlockSpec(memory_space=pltpu.VMEM)
    return pl.pallas_call(
        combine_kernel,
        out_shape=[jax.ShapeDtypeStruct((SUB, width), jnp.float32)] * len(TURNS),
        in_specs=[pl.BlockSpec(memory_space=pltpu.SMEM)] + [vmem] * len(TURNS),
        out_specs=[vmem] * len(TURNS),
        compiler_params=pltpu.CompilerParams(vmem_limit_bytes=SMALL_BYTES),
        name="combine",
    )(spot, *parts)


def finish_kernel(paths_total, *refs):
    parts, (reserve_ref, fine_ref, corr_ref) = refs[:-3], refs[-3:]
    products = reserve_ref.shape[1]
    width = parts[0].shape[1]
    half = len(parts) // 2
    mine, theirs = None, None
    for turn, part in zip(FAR_TURNS, parts):
        if turn < half:
            mine = part[...] if mine is None else mine + part[...]
        else:
            theirs = part[...] if theirs is None else theirs + part[...]
    reserve = reserve_ref[...]
    limit = jnp.concatenate([reserve] * (width // products), axis=1)
    scale = 1.0 / paths_total
    fine = jnp.maximum((mine + theirs) * scale - limit, 0.0)
    coarse = 0.5 * (
        jnp.maximum(mine * (2.0 * scale) - limit, 0.0)
        + jnp.maximum(theirs * (2.0 * scale) - limit, 0.0)
    )
    gap = fine - coarse

    def over_steps(term):
        lanes = 2 * products
        total = term[:, :lanes]
        for start in range(lanes, width, lanes):
            total = total + term[:, start : start + lanes]
        return (total[:, :products] + total[:, products:]) * (products / width)

    fine_ref[...] = over_steps(fine)
    corr_ref[...] = over_steps(gap)


def per_device(
    increments,
    outer_shock,
    outer_vol,
    factor_vol,
    factor_mix,
    leg_factor,
    leg_weight,
    strike,
    reserve,
):
    step_count, _, paths_here, scen_rows = increments.shape
    path_count = lax.axis_size("path")
    paths_total = paths_here * path_count
    spot = lax.axis_index("path").astype(jnp.int32).reshape(1)

    def swap(value, distance):
        if distance == 0:
            return value
        return lax.ppermute(value, "path", [(i, i ^ distance) for i in range(path_count)])

    own = outer_shock.T
    shared = {turn: swap(own, turn) for turn in ARRIVE}
    mix_w, shared[0], vol, val_w, drift, strike_wide = prepare(
        step_count, scen_rows, own, outer_vol, factor_vol, factor_mix, leg_factor, leg_weight, strike
    )
    rows = relay(spot, vol, [shared[turn] for turn in ARRIVE])
    stacks = [swap(rows, turn * NEAR) for turn in ARRIVE_FAR]
    early = ahead(increments, mix_w, rows)
    local = simulate(spot, increments, stacks, early, (mix_w, val_w, drift, strike_wide))
    parts = [swap(value, turn) for value, turn in zip(local, TURNS)]
    sums = combine(spot, parts)
    pieces = [swap(value, turn * NEAR) for value, turn in zip(sums, FAR_TURNS)]
    out = jax.ShapeDtypeStruct(reserve.shape, jnp.float32)
    return pl.pallas_call(
        functools.partial(finish_kernel, paths_total),
        out_shape=(out, out),
        compiler_params=pltpu.CompilerParams(vmem_limit_bytes=SMALL_BYTES),
        name="finish",
    )(*pieces, reserve)


def solution(mesh):
    in_specs = (
        P(None, None, "path", "scen"),
        P(None, ("scen", "path")),
        P(),
        P(),
        P(),
        P(),
        P(),
        P(),
        P(("scen", "path"), None),
    )
    out_specs = (P(("scen", "path"), None), P(("scen", "path"), None))
    return jax.shard_map(
        per_device, mesh=mesh, in_specs=in_specs, out_specs=out_specs, check_vma=False
    )
```
